128 devices in a mesh: dp: 32 (over z, x, y_hi), row: 2 (over core), col: 2 (over y_lo).
Axes of the slice: x: 4, y: 4 (y_hi: 2, y_lo: 2; y = y_hi * 2 + y_lo), z: 4, core: 2. Of those that a mesh axis runs over, the one named last changes fastest.
Arguments:
- tokens: bfloat16 [16384, 768], P(('dp', 'col'), 'row'), may hold values from -6 to 6
- cotangent: bfloat16 [16384, 768], P(('dp', 'col'), 'row'), may hold values from -6 to 6
- ln1_gain: float32 [2, 768], P(None, 'row'), may hold values from 0.1 to 1.9
- ln1_bias: float32 [2, 768], P(None, 'row'), may hold values from -1.75 to 1.75
- w_qkv: bfloat16 [2, 768, 3, 768], P(None, 'row', None, 'col'), may hold values from -0.25 to 0.25
- qv_bias: float32 [2, 2, 768], P(None, None, 'col'), may hold values from -1.75 to 1.75
- w_out: bfloat16 [2, 768, 768], P(None, 'col', 'row'), may hold values from -0.625 to 0.625
- b_out: float32 [2, 768], P(None, 'row'), may hold values from -1.75 to 1.75
- ln2_gain: float32 [2, 768], P(None, 'row'), may hold values from 0.1 to 1.9
- ln2_bias: float32 [2, 768], P(None, 'row'), may hold values from -1.75 to 1.75
- w_up: bfloat16 [2, 768, 3072], P(None, 'row', 'col'), may hold values from -0.21875 to 0.21875
- b_up: float32 [2, 3072], P(None, 'col'), may hold values from -1.75 to 1.75
- w_down: bfloat16 [2, 3072, 768], P(None, 'col', 'row'), may hold values from -0.109375 to 0.109375
- b_down: float32 [2, 768], P(None, 'row'), may hold values from -1.75 to 1.75
- seq_lengths: int32 [128], replicated, may hold values from 0 to 512, as said below
- seq_owner: int32 [128], replicated, may hold values from 0 to 31
- seq_offset: int32 [128], replicated, may hold values from 0 to 512, as said below
Outputs:
- out_act: float32 [16384, 768], P(('dp', 'col'), 'row')
- grad_tokens: float32 [16384, 768], P(('dp', 'col'), 'row')
- grad_ln1_gain: float32 [2, 768], P(None, 'row')
- grad_ln1_bias: float32 [2, 768], P(None, 'row')
- grad_w_qkv: float32 [2, 768, 3, 768], P(None, 'row', None, 'col')
- grad_qv_bias: float32 [2, 2, 768], P(None, None, 'col')
- grad_w_out: float32 [2, 768, 768], P(None, 'col', 'row')
- grad_b_out: float32 [2, 768], P(None, 'row')
- grad_ln2_gain: float32 [2, 768], P(None, 'row')
- grad_ln2_bias: float32 [2, 768], P(None, 'row')
- grad_w_up: float32 [2, 768, 3072], P(None, 'row', 'col')
- grad_b_up: float32 [2, 3072], P(None, 'col')
- grad_w_down: float32 [2, 3072, 768], P(None, 'col', 'row')
- grad_b_down: float32 [2, 768], P(None, 'row')
The draws below stay inside these ranges and needn't reach their ends.
Inputs may be any that keep to these rules, and one draw needn't show every extreme that they name: `seq_lengths`: each data index owns 4 of the sequences. Its sequences lie end to end from its first position in the order of their offsets and cover more than three quarters of its 512 positions; the positions after them belong to no sequence. One sequence of each data index covers its two middle positions, and some sequence has exactly 512 tokens. `seq_offset`: offsets count positions within the owner's 512 positions; a sequence of zero tokens may start at 512.
All inputs are finite; a program needn't handle non-finite values.
Results may differ from the reference program's by a relative error of at most 0.014.
Values may be sent and summed in bfloat16 or wider, within the bound.
No kernel may reach another device: no remote copies, remote signals or barrier semaphores. Data moves between devices by JAX's collectives and lax.ppermute only.
A program may use at most 128 MiB of HBM per device.

```python
import jax
import jax.numpy as jnp
from jax import lax

D = 768
H = 12
DH = 64
FF = 3072
LAYERS = 2
SLOTS = 4
TOK_G = 512
TOKENS = 16384
N_DP = 32


def packing(key):
    key_used, key_full, key_rest, key_parts, key_long, key_shuffle = jax.random.split(key, 6)
    groups = jnp.arange(N_DP, dtype=jnp.int32)
    slot_index = jnp.arange(SLOTS, dtype=jnp.int32)
    used_tokens = jax.random.randint(key_used, (N_DP,), 3 * TOK_G // 4 + 1, TOK_G + 1, dtype=jnp.int32)
    full_group = jax.random.randint(key_full, (), 0, N_DP, dtype=jnp.int32)
    is_full = groups == full_group
    used_tokens = jnp.where(is_full, TOK_G, used_tokens)
    rest_tokens = jax.random.randint(key_rest, (N_DP,), 0, TOK_G // 4 + 1, dtype=jnp.int32)
    rest_tokens = jnp.where(is_full, 0, rest_tokens)
    long_slot = jax.random.randint(key_long, (N_DP,), 0, SLOTS, dtype=jnp.int32)
    is_long = slot_index[None, :] == long_slot[:, None]
    portions = jax.random.randint(key_parts, (N_DP, SLOTS), 1, 9, dtype=jnp.int32)
    portions = jnp.where(is_long, 0, portions)
    others = portions * rest_tokens[:, None] // jnp.sum(portions, axis=1, keepdims=True)
    lengths = jnp.where(is_long, (used_tokens - jnp.sum(others, axis=1))[:, None], others)
    offsets = jnp.cumsum(lengths, axis=1) - lengths
    owners = jnp.repeat(groups, SLOTS)
    shuffle = jax.random.permutation(key_shuffle, N_DP * SLOTS)
    return (lengths.reshape(-1)[shuffle].astype(jnp.int32), owners[shuffle].astype(jnp.int32), offsets.reshape(-1)[shuffle].astype(jnp.int32))


def draw_seq_lengths(key, part):
    lengths, owners, offsets = packing(key)
    return lengths


def draw_seq_owner(key, part):
    lengths, owners, offsets = packing(key)
    return owners


def draw_seq_offset(key, part):
    lengths, owners, offsets = packing(key)
    return offsets


def drawn_values(key, shape, deviation):
    return deviation * jax.random.truncated_normal(key, -6.0, 6.0, shape, jnp.float32)


def draw_tokens(key, part):
    key = jax.random.fold_in(key, 11)
    values = drawn_values(key, (TOKENS, D), 1.0)
    return values.astype(jnp.bfloat16)


def draw_cotangent(key, part):
    key = jax.random.fold_in(key, 12)
    values = drawn_values(key, (TOKENS, D), 1.0)
    return values.astype(jnp.bfloat16)


def draw_w_qkv(key, part):
    key = jax.random.fold_in(key, 13)
    deviation = D ** (-0.5)
    values = drawn_values(key, (LAYERS, D, 3, D), deviation)
    return jnp.clip(values, -0.25, 0.25).astype(jnp.bfloat16)


def level_of(stream_key, shape, cuts, low, high):
    def one(dim, blocks):
        draws = jax.random.uniform(jax.random.fold_in(jax.random.fold_in(stream_key, 6), dim), (blocks,), jnp.float32, low / len(cuts), high / len(cuts))
        return jnp.repeat(jnp.exp(draws), shape[dim] // blocks).reshape((-1,) + (1,) * (len(shape) - dim - 1))

    level = one(*cuts[0])
    for cut in cuts[1:]:
        level = level * one(*cut)
    return level


def scatter_about(stream_key, extent, scale, most, cuts=(), kind=jnp.bfloat16):
    gain = level_of(stream_key, extent, cuts, -0.22, 0.18) if cuts else 1.0
    values = jax.random.normal(stream_key, extent, jnp.float32) * scale * gain
    return jnp.minimum(jnp.maximum(values, -most), most).astype(kind)


def setup_inputs(seed: int = 0) -> dict:
    key_of = jax.random.split(jax.random.key(seed), 18)
    return {
        "tokens": draw_tokens(jax.random.fold_in(key_of[17], 71), 0),
        "cotangent": draw_cotangent(jax.random.fold_in(key_of[17], 71), 0),
        "ln1_gain": jnp.clip(1.0 + 0.18 * jax.random.normal(key_of[2], (LAYERS, D), jnp.float32), 0.1, 1.9),
        "ln1_bias": scatter_about(key_of[3], (LAYERS, D), 0.3, 1.75, ((1, 2),), jnp.float32),
        "w_qkv": draw_w_qkv(jax.random.fold_in(key_of[17], 71), 0),
        "qv_bias": scatter_about(key_of[5], (LAYERS, 2, D), 0.3, 1.75, ((2, 2),), jnp.float32),
        "w_out": scatter_about(key_of[6], (LAYERS, D, D), (D // 8) ** -0.5, 0.625, ((1, 2), (2, 2))),
        "b_out": scatter_about(key_of[7], (LAYERS, D), 0.3, 1.75, ((1, 2),), jnp.float32),
        "ln2_gain": jnp.clip(1.0 + 0.18 * jax.random.normal(key_of[8], (LAYERS, D), jnp.float32), 0.1, 1.9),
        "ln2_bias": scatter_about(key_of[9], (LAYERS, D), 0.3, 1.75, ((1, 2),), jnp.float32),
        "w_up": scatter_about(key_of[10], (LAYERS, D, FF), D ** -0.5, 0.21875, ((1, 2), (2, 2))),
        "b_up": scatter_about(key_of[11], (LAYERS, FF), 0.3, 1.75, ((1, 2),), jnp.float32),
        "w_down": scatter_about(key_of[12], (LAYERS, FF, D), FF ** -0.5, 0.109375, ((1, 2), (2, 2))),
        "b_down": scatter_about(key_of[13], (LAYERS, D), 0.3, 1.75, ((1, 2),), jnp.float32),
        "seq_lengths": draw_seq_lengths(jax.random.fold_in(key_of[17], 71), 0),
        "seq_owner": draw_seq_owner(jax.random.fold_in(key_of[17], 71), 0),
        "seq_offset": draw_seq_offset(jax.random.fold_in(key_of[17], 71), 0),
    }


@jax.custom_vjp
def low(v):
    return lax.optimization_barrier(v.astype(jnp.bfloat16)).astype(jnp.float32)

@jax.custom_vjp
def low_back(v):
    return v

def low_keep(v):
    return (low(v), None)

def low_pass(kept, grad):
    return (grad,)

def back_keep(v):
    return (v, None)

def back_low(kept, grad):
    return (low(grad),)
low.defvjp(low_keep, low_pass)
low_back.defvjp(back_keep, back_low)
HIGHEST = lax.Precision.HIGHEST
EPSILON = 1e-05
MASKED_SCORE = -1e+30

def segment_ids(group_index, seq_lengths, seq_owner, seq_offset, token_count):
    position = jnp.arange(token_count, dtype=jnp.int32)[:, None]
    inside = (seq_owner[None, :] == group_index) & (position >= seq_offset[None, :]) & (position < seq_offset[None, :] + seq_lengths[None, :])
    numbers = jnp.arange(seq_lengths.shape[0], dtype=jnp.int32)[None, :] + 1
    return (lax.optimization_barrier(jnp.sum(jnp.where(inside, numbers, 0), axis=1)) - 1).astype(jnp.int32)

def allowed(seg_query, pos_query, seg_key, pos_key):
    same_seq = (seg_query[:, None] == seg_key[None, :]) & (seg_query[:, None] >= 0)
    causal = pos_key[None, :] <= pos_query[:, None]
    return same_seq & causal | (pos_key[None, :] == pos_query[:, None])

def layer_norm(inputs, gain_row, bias_row):
    center = lax.optimization_barrier(jnp.mean(inputs, axis=-1, keepdims=True))
    spread = lax.optimization_barrier(jnp.mean(inputs * inputs, axis=-1, keepdims=True)) - center * center
    return (inputs - center) * lax.rsqrt(spread + EPSILON) * gain_row + bias_row

def attend(pieces):
    queries, key_rows, values, segments = pieces
    position = jnp.arange(queries.shape[0], dtype=jnp.int32)
    allow_mask = allowed(segments, position, segments, position)
    score_scale = queries.shape[2] ** (-0.5)
    scores = low_back(jnp.einsum('qhe,khe->hqk', queries, key_rows, precision=HIGHEST) * score_scale)
    scores = jnp.where(allow_mask[None], scores, MASKED_SCORE)
    weights = low(jax.nn.softmax(scores, axis=-1))
    return jnp.einsum('hqk,khe->qhe', weights, values, precision=HIGHEST)

def forward(hidden, ln1_gain, ln1_bias, w_qkv, qv_bias, w_out, b_out, ln2_gain, ln2_bias, w_up, b_up, w_down, b_down, segments):
    groups, group_tokens = segments.shape
    model_width = hidden.shape[1]
    shape_split = (groups, group_tokens, H, DH)
    for layer_index in range(LAYERS):
        normed = low(layer_norm(hidden, ln1_gain[layer_index], ln1_bias[layer_index]))
        project = jnp.einsum('td,dkf->tkf', normed, w_qkv[layer_index], precision=HIGHEST)
        queries = low_back(low(project[:, 0] + qv_bias[layer_index, 0]))
        key_rows = low_back(low(project[:, 1]))
        values = low_back(low(project[:, 2] + qv_bias[layer_index, 1]))
        mixture = lax.map(jax.checkpoint(attend), (queries.reshape(shape_split), key_rows.reshape(shape_split), values.reshape(shape_split), segments))
        mixture = low_back(low(mixture.reshape(hidden.shape[0], model_width)))
        hidden = hidden + low_back(jnp.dot(mixture, w_out[layer_index], precision=HIGHEST) + b_out[layer_index])
        normed = low(layer_norm(hidden, ln2_gain[layer_index], ln2_bias[layer_index]))
        upward = low_back(jnp.dot(normed, w_up[layer_index], precision=HIGHEST) + b_up[layer_index])
        activated = low(jax.nn.gelu(upward, approximate=False))
        hidden = hidden + low_back(jnp.dot(activated, w_down[layer_index], precision=HIGHEST) + b_down[layer_index])
    return hidden

def reference(tokens, cotangent, ln1_gain, ln1_bias, w_qkv, qv_bias, w_out, b_out, ln2_gain, ln2_bias, w_up, b_up, w_down, b_down, seq_lengths, seq_owner, seq_offset):

    def group_segments(group_index):
        return segment_ids(group_index, seq_lengths, seq_owner, seq_offset, TOK_G)
    segments = jax.vmap(group_segments)(jnp.arange(N_DP, dtype=jnp.int32))
    params = tuple((argument.astype(jnp.float32) for argument in (ln1_gain, ln1_bias, w_qkv, qv_bias, w_out, b_out, ln2_gain, ln2_bias, w_up, b_up, w_down, b_down)))

    def run_layers(hidden, *weights):
        return forward(hidden, *weights, segments)
    outputs, pullback = jax.vjp(run_layers, tokens.astype(jnp.float32), *params)
    gradients = pullback(cotangent.astype(jnp.float32))
    return (outputs, gradients[0], gradients[1], gradients[2], gradients[3], gradients[4], gradients[5], gradients[6], gradients[7], gradients[8], gradients[9], gradients[10], gradients[11], gradients[12])
```

```python
import jax
import jax.numpy as jnp
from jax import lax
from jax.experimental import pallas as pl
from jax.experimental.pallas import tpu as pltpu
from jax.sharding import PartitionSpec as P

DH = 64
LAYERS = 2
EPSILON = 1e-05
MASKED_SCORE = -1e30
INV_SQRT2 = 0.7071067811865476
INV_SQRT2PI = 0.3989422804014327
BF = jnp.bfloat16
F32 = jnp.float32
VMEM_BYTES = 48 * 1024 * 1024


def call(kernel, ins, outs, flops=0, specs=None):
    in_specs = []
    for position, operand in enumerate(ins):
        spec = (specs or {}).get(position)
        in_specs.append(spec if spec is not None else whole_spec(operand))
    size = sum(x.size * x.dtype.itemsize for x in ins) + sum(
        x.size * x.dtype.itemsize for x in outs
    )
    return pl.pallas_call(
        kernel,
        out_shape=outs,
        in_specs=in_specs,
        out_specs=[whole_spec(x) for x in outs],
        grid=(1,),
        compiler_params=pltpu.CompilerParams(vmem_limit_bytes=VMEM_BYTES),
        cost_estimate=pl.CostEstimate(flops=flops, bytes_accessed=size, transcendentals=0),
    )(*ins)


def whole_spec(operand):
    zeros = (0,) * len(operand.shape)
    return pl.BlockSpec(operand.shape, lambda i: zeros)


def layer_spec(operand, layer):
    rest = operand.shape[1:]
    zeros = (0,) * len(rest)
    return pl.BlockSpec((None,) + rest, lambda i: (layer,) + zeros)


def shape_of(shape, dtype):
    return jax.ShapeDtypeStruct(shape, dtype)


def mm(left, right):
    return jnp.dot(left, right, preferred_element_type=F32)


def mm_nt(left, right):
    return lax.dot_general(left, right, (((1,), (1,)), ((), ())), preferred_element_type=F32)


def mm_tn(left, right):
    return lax.dot_general(left, right, (((0,), (0,)), ((), ())), preferred_element_type=F32)


def swapped(ref):
    half = ref.shape[0] // 2
    return jnp.concatenate([ref[half:, :], ref[:half, :]], axis=0).astype(F32)


def both(own_ref, received_ref):
    return own_ref[...].astype(F32) + swapped(received_ref)


def statistics(inputs):
    center = jnp.mean(inputs, axis=1, keepdims=True)
    second = jnp.mean(inputs * inputs, axis=1, keepdims=True)
    inverse = lax.rsqrt(second - center * center + EPSILON)
    return (inputs - center) * inverse, inverse


def norm_grad(grad_norm, normal, inverse, gain):
    scaled = grad_norm * gain
    first = jnp.mean(scaled, axis=1, keepdims=True)
    second = jnp.mean(scaled * normal, axis=1, keepdims=True)
    return inverse * (scaled - first - normal * second)


def col_sum(values):
    return jnp.sum(values.astype(F32), axis=0, keepdims=True)


def pieces(own_ref, row_ref, col_ref):
    mine = jnp.concatenate([own_ref[...], row_ref[...]], axis=1)
    return jnp.concatenate([mine, col_ref[...]], axis=0).astype(F32)


def qkv_part(hidden, gain, bias, w_own, w_oth, qvb_ref, x_ref, a_own, a_oth, q_ref, kv_ref):
    x_ref[...] = hidden
    normal, _ = statistics(hidden)
    normed = (normal * gain + bias).astype(BF)
    half = normed.shape[1] // 2
    left, right = normed[:, :half], normed[:, half:]
    a_own[...] = left
    a_oth[...] = right
    width = q_ref.shape[1]
    q_ref[...] = (mm(left, w_own[0]) + mm(right, w_oth[0]) + qvb_ref[0:1, :]).astype(BF)
    kv_ref[:, :width] = (mm(left, w_own[1]) + mm(right, w_oth[1])).astype(BF)
    kv_ref[:, width:] = (mm(left, w_own[2]) + mm(right, w_oth[2]) + qvb_ref[1:2, :]).astype(BF)


def first_kernel(own, row, col, par, qvb, w_own, w_oth, *outs):
    hidden = pieces(own, row, col)
    qkv_part(hidden, par[0:1, :], par[1:2, :], w_own, w_oth, qvb, *outs)


def next_kernel(x1, y_own, y_rec, par_before, par, qvb, w_own, w_oth, *outs):
    hidden = x1[...] + (both(y_own, y_rec) + par_before[5:6, :])
    qkv_part(hidden, par[0:1, :], par[1:2, :], w_own, w_oth, qvb, *outs)


def attention_mask(info, seq_len, seq_own, seq_off, rows, cols):
    quarter = rows // 2
    i = lax.broadcasted_iota(jnp.int32, (rows, 1), 0)
    j = lax.broadcasted_iota(jnp.int32, (1, cols), 1)
    pos_q = jnp.where(i < quarter, info[1] + i, info[2] + i - quarter)
    pos_k = jnp.where(
        j < 2 * quarter,
        jnp.where(j < quarter, info[1] + j, info[2] + j - quarter),
        jnp.where(j < 3 * quarter, info[3] + j - 2 * quarter, info[4] + j - 3 * quarter),
    )
    offset = seq_off[...]
    inside = (
        (seq_own[...] == info[0]) & (pos_q >= offset) & (pos_q < offset + seq_len[...])
    )
    start = jnp.max(jnp.where(inside, offset, -1), axis=1, keepdims=True)
    start = jnp.where(start < 0, pos_q, start)
    return (pos_k <= pos_q) & (pos_k >= start)


def head_lanes(rows, which):
    lane = lax.broadcasted_iota(jnp.int32, (rows, 2 * DH), 1)
    return (lane < DH) if which == 0 else (lane >= DH)


def attend_kernel(
    info, seq_len, seq_own, seq_off, q, kv_own, kv_oth, w_own, w_oth, o_ref, lse_ref, y_ref
):
    rows, width = q.shape
    mask = attention_mask(info, seq_len, seq_own, seq_off, rows, 2 * rows)
    sides = [head_lanes(rows, 0), head_lanes(rows, 1)]
    lane = lax.broadcasted_iota(jnp.int32, (rows, 128), 1)
    logs = jnp.zeros((rows, 128), F32)
    scale = DH**-0.5
    for pair in range(width // (2 * DH)):
        span = slice(pair * 2 * DH, (pair + 1) * 2 * DH)
        vspan = slice(width + pair * 2 * DH, width + (pair + 1) * 2 * DH)
        queries = q[:, span] * jnp.asarray(scale, BF)
        keys = jnp.concatenate([kv_own[:, span], kv_oth[:, span]], axis=0)
        values = jnp.concatenate([kv_own[:, vspan], kv_oth[:, vspan]], axis=0)
        mixed = None
        for side in range(2):
            scores = mm_nt(jnp.where(sides[side], queries, jnp.zeros_like(queries)), keys)
            scores = jnp.where(mask, scores, MASKED_SCORE)
            largest = jnp.max(scores, axis=1, keepdims=True)
            powers = jnp.exp(scores - largest)
            total = jnp.sum(powers, axis=1, keepdims=True)
            out = mm((powers * (1.0 / total)).astype(BF), values)
            logs = jnp.where(lane == 2 * pair + side, largest + jnp.log(total), logs)
            mixed = out if side == 0 else jnp.where(sides[0], mixed, out)
        o_ref[:, span] = mixed.astype(BF)
    lse_ref[...] = logs
    mixture = o_ref[...]
    half = y_ref.shape[1] // 2
    y_ref[:, :half] = mm(mixture, w_own[...]).astype(BF)
    y_ref[:, half:] = mm(mixture, w_oth[...]).astype(BF)


def mlp_kernel(
    x, y_own, y_rec, par, bup, wu_own, wu_oth, wd_own, wd_oth,
    x1_ref, m_own, m_oth, h_ref, gp_ref, y_ref,
):
    middle = x[...] + (both(y_own, y_rec) + par[2:3, :])
    x1_ref[...] = middle
    normal, _ = statistics(middle)
    normed = (normal * par[3:4, :] + par[4:5, :]).astype(BF)
    half = normed.shape[1] // 2
    left, right = normed[:, :half], normed[:, half:]
    m_own[...] = left
    m_oth[...] = right
    width = h_ref.shape[1]
    step = 384
    out_own = out_oth = None
    for at in range(0, width, step):
        span = slice(at, at + step)
        upward = mm(left, wu_own[:, span]) + mm(right, wu_oth[:, span]) + bup[:, span]
        phi = 0.5 + 0.5 * lax.erf(upward * INV_SQRT2)
        density = jnp.exp(-0.5 * upward * upward) * INV_SQRT2PI
        active = (upward * phi).astype(BF)
        h_ref[:, span] = active
        gp_ref[:, span] = (phi + upward * density).astype(BF)
        part_own = mm(active, wd_own[span, :])
        part_oth = mm(active, wd_oth[span, :])
        out_own = part_own if out_own is None else out_own + part_own
        out_oth = part_oth if out_oth is None else out_oth + part_oth
    y_ref[:, :half] = out_own.astype(BF)
    y_ref[:, half:] = out_oth.astype(BF)


def mlp_back(
    grad, gp, wu_own, wu_oth, wd_own, wd_oth,
    g_ref, gy_own, gy_oth, du_ref, dm_ref, sdown_ref, sup_ref,
):
    g_ref[...] = grad
    branch = grad.astype(BF)
    half = branch.shape[1] // 2
    left, right = branch[:, :half], branch[:, half:]
    gy_own[...] = left
    gy_oth[...] = right
    sdown_ref[...] = col_sum(branch)
    width = gp.shape[1]
    step = 384
    out_own = out_oth = None
    for at in range(0, width, step):
        span = slice(at, at + step)
        grad_active = mm_nt(left, wd_own[span, :]) + mm_nt(right, wd_oth[span, :])
        grad_up = (grad_active * gp[:, span].astype(F32)).astype(BF)
        du_ref[:, span] = grad_up
        sup_ref[:, span] = col_sum(grad_up)
        part_own = mm_nt(grad_up, wu_own[:, span])
        part_oth = mm_nt(grad_up, wu_oth[:, span])
        out_own = part_own if out_own is None else out_own + part_own
        out_oth = part_oth if out_oth is None else out_oth + part_oth
    dm_ref[:, :half] = out_own.astype(BF)
    dm_ref[:, half:] = out_oth.astype(BF)


def last_back_kernel(own, row, col, gp, wu_own, wu_oth, wd_own, wd_oth, *outs):
    mlp_back(pieces(own, row, col), gp, wu_own, wu_oth, wd_own, wd_oth, *outs)


def input_grad(g1, da_own, da_rec, x, par, small_ref):
    grad_normed = both(da_own, da_rec)
    normal, inverse = statistics(x[...])
    small_ref[0:1, :] = col_sum(grad_normed * normal)
    small_ref[1:2, :] = col_sum(grad_normed)
    return g1[...] + norm_grad(grad_normed, normal, inverse, par[0:1, :])


def next_back_kernel(
    g1, da_own, da_rec, x, par, gp, wu_own, wu_oth, wd_own, wd_oth, small_ref, *outs
):
    grad = input_grad(g1, da_own, da_rec, x, par, small_ref)
    mlp_back(grad, gp, wu_own, wu_oth, wd_own, wd_oth, *outs)


def end_back_kernel(g1, da_own, da_rec, x, par, small_ref, own_ref, oth_ref):
    grad = input_grad(g1, da_own, da_rec, x, par, small_ref)
    rows, width = grad.shape
    own_ref[...] = grad[: rows // 2, : width // 2]
    oth_ref[...] = grad[: rows // 2, width // 2 :]


def attend_back_kernel(
    info, seq_len, seq_own, seq_off, grad, dm_own, dm_rec, x1, par, w_own, w_oth,
    q, kv_own, kv_oth, lse,
    g1_ref, ga_own, ga_oth, dq_ref, dkv_own, dkv_oth, small_ref,
):
    grad_normed = both(dm_own, dm_rec)
    normal, inverse = statistics(x1[...])
    grad_middle = grad[...] + norm_grad(grad_normed, normal, inverse, par[3:4, :])
    g1_ref[...] = grad_middle
    branch = grad_middle.astype(BF)
    small_ref[0:1, :] = col_sum(branch)
    small_ref[1:2, :] = col_sum(grad_normed * normal)
    small_ref[2:3, :] = col_sum(grad_normed)
    half = branch.shape[1] // 2
    left, right = branch[:, :half], branch[:, half:]
    ga_own[...] = left
    ga_oth[...] = right
    grad_mixed = (mm_nt(left, w_own[...]) + mm_nt(right, w_oth[...])).astype(BF)
    rows, width = q.shape
    mask = attention_mask(info, seq_len, seq_own, seq_off, rows, 2 * rows)
    sides = [head_lanes(rows, 0), head_lanes(rows, 1)]
    key_sides = head_lanes(2 * rows, 0)
    scale = DH**-0.5
    for pair in range(width // (2 * DH)):
        span = slice(pair * 2 * DH, (pair + 1) * 2 * DH)
        vspan = slice(width + pair * 2 * DH, width + (pair + 1) * 2 * DH)
        queries = q[:, span] * jnp.asarray(scale, BF)
        keys = jnp.concatenate([kv_own[:, span], kv_oth[:, span]], axis=0)
        values = jnp.concatenate([kv_own[:, vspan], kv_oth[:, vspan]], axis=0)
        grad_out = grad_mixed[:, span]
        grad_q = grad_k = grad_v = None
        for side in range(2):
            head = 2 * pair + side
            scores = mm_nt(jnp.where(sides[side], queries, jnp.zeros_like(queries)), keys)
            scores = jnp.where(mask, scores, MASKED_SCORE)
            probability = jnp.exp(scores - lse[:, head : head + 1])
            grad_prob = mm_nt(jnp.where(sides[side], grad_out, jnp.zeros_like(grad_out)), values)
            inner = jnp.sum(grad_prob * probability, axis=1, keepdims=True)
            grad_scores = (probability * (grad_prob - inner)).astype(BF)
            part_q = mm(grad_scores, keys)
            part_k = mm_tn(grad_scores, queries)
            part_v = mm_tn(probability.astype(BF), grad_out)
            if side == 0:
                grad_q, grad_k, grad_v = part_q, part_k, part_v
            else:
                grad_q = jnp.where(sides[0], grad_q, part_q)
                grad_k = jnp.where(key_sides, grad_k, part_k)
                grad_v = jnp.where(key_sides, grad_v, part_v)
        dq_ref[:, span] = (grad_q * scale).astype(BF)
        dkv_own[:, span] = grad_k[:rows].astype(dkv_own.dtype)
        dkv_oth[:, span] = grad_k[rows:].astype(dkv_oth.dtype)
        dkv_own[:, vspan] = grad_v[:rows].astype(dkv_own.dtype)
        dkv_oth[:, vspan] = grad_v[rows:].astype(dkv_oth.dtype)


def project_back_kernel(dq, dkv_own, dkv_rec, w_own, w_oth, da_ref, dkv_ref, small_ref):
    width = dq.shape[1]
    total = (dkv_own[...].astype(F32) + dkv_rec[...].astype(F32)).astype(BF)
    dkv_ref[...] = total
    small_ref[0:1, :] = col_sum(dq[...])
    small_ref[1:2, :] = col_sum(total[:, width:])
    parts = (dq[...], total[:, :width], total[:, width:])
    half = da_ref.shape[1] // 2
    for at, weight in ((0, w_own), (half, w_oth)):
        out = mm_nt(parts[0], weight[0]) + mm_nt(parts[1], weight[1]) + mm_nt(parts[2], weight[2])
        da_ref[:, at : at + half] = out.astype(BF)


def weight_grad_kernel(
    h_own, h_rec, gy_own, gy_rec, m_own, m_rec, du_own, du_rec,
    o_own, o_rec, ga_own, ga_rec, a_own, a_rec, dq_own, dq_rec, dkv_own, dkv_rec,
    out_ref,
):
    def term(left_own, left_rec, right_own, right_rec):
        return (mm_tn(left_own, right_own) + mm_tn(left_rec, right_rec)).astype(BF)

    size = gy_own.shape[1]
    at = 0
    for span in (slice(k * size, (k + 1) * size) for k in range(4)):
        out_ref[at : at + size, :] = term(h_own[:, span], h_rec[:, span], gy_own[...], gy_rec[...])
        at += size
    for span in (slice(k * size, (k + 1) * size) for k in range(4)):
        out_ref[at : at + size, :] = term(m_own[...], m_rec[...], du_own[:, span], du_rec[:, span])
        at += size
    out_ref[at : at + size, :] = term(a_own[...], a_rec[...], dq_own[...], dq_rec[...])
    at += size
    for span in (slice(k * size, (k + 1) * size) for k in range(2)):
        out_ref[at : at + size, :] = term(
            a_own[...], a_rec[...], dkv_own[:, span], dkv_rec[:, span]
        )
        at += size
    out_ref[at : at + size, :] = term(o_own[...], o_rec[...], ga_own[...], ga_rec[...])


SWAP = [(0, 1), (1, 0)]


def row_swap(operand):
    return lax.ppermute(operand, "row", SWAP)


def col_swap(operand):
    return lax.ppermute(operand, "col", SWAP)


def flipped(index, pairing):
    z, x, y = index // 8, (index // 2) % 4, index % 2
    if pairing == "za":
        z ^= 1
    elif pairing == "zb":
        z = 3 - z
    elif pairing == "xa":
        x ^= 1
    elif pairing == "xb":
        x = 3 - x
    else:
        y ^= 1
    return z * 8 + x * 2 + y


def side_of(index, pairing):
    z, x, y = index // 8, (index // 2) % 4, index % 2
    return {
        "za": (z + 1) // 2 % 2,
        "zb": z // 2,
        "xa": (x + 1) // 2 % 2,
        "xb": x // 2,
        "y": y,
    }[pairing]


def exchange(operand, pairings):
    table = [
        (dp * 2 + row, flipped(dp, pairings[row]) * 2 + row) for dp in range(32) for row in range(2)
    ]
    return lax.ppermute(operand, ("dp", "row"), table)


def my_side(pairings):
    dp = lax.axis_index("dp")
    return jnp.where(
        lax.axis_index("row") == 0, side_of(dp, pairings[0]), side_of(dp, pairings[1])
    )


def halve(operand, pairings):
    half = operand.shape[0] // 2
    side = my_side(pairings)
    sent = lax.dynamic_slice_in_dim(operand, (1 - side) * half, half, 0).astype(BF)
    kept = lax.dynamic_slice_in_dim(operand, side * half, half, 0).astype(F32)
    return kept + exchange(sent, pairings).astype(F32)


def double(operand, pairings):
    other = exchange(operand, pairings)
    return jnp.where(
        my_side(pairings) == 0,
        jnp.concatenate([operand, other]),
        jnp.concatenate([other, operand]),
    )


ORDER_ONE = [("za", "xa"), ("xa", "za"), ("zb", "xb"), ("xb", "zb")]
ORDER_TWO = [("zb", "xb"), ("xb", "zb"), ("za", "xa"), ("xa", "za")]
ACROSS = ("y", "y")


def data_total(operand):
    half = operand.shape[0] // 2
    one, two = operand[:half], operand[half:]
    for step in range(4):
        one = halve(one, ORDER_ONE[step])
        two = halve(two, ORDER_TWO[step])
    joined = halve(jnp.concatenate([one, two]), ACROSS).astype(BF)
    joined = double(joined, ACROSS)
    half = joined.shape[0] // 2
    one, two = joined[:half], joined[half:]
    for step in reversed(range(4)):
        one = double(one, ORDER_ONE[step])
        two = double(two, ORDER_TWO[step])
    return jnp.concatenate([one, two])


def small_total(operand):
    for pairing in ("za", "xa", "zb", "xb", "y"):
        operand = operand + exchange(operand, (pairing, pairing))
    return operand


def body(
    tokens,
    cotangent,
    ln1_gain,
    ln1_bias,
    w_qkv,
    qv_bias,
    w_out,
    b_out,
    ln2_gain,
    ln2_bias,
    w_up,
    b_up,
    w_down,
    b_down,
    seq_lengths,
    seq_owner,
    seq_offset,
):
    row = lax.axis_index("row")
    col = lax.axis_index("col")
    block, half = tokens.shape
    part = block // 2
    rows = block
    width = 2 * half
    hidden_part = w_up.shape[2]

    def split_input(operand):
        own = lax.dynamic_slice_in_dim(operand, row * part, part, 0)
        sent = lax.dynamic_slice_in_dim(operand, (1 - row) * part, part, 0)
        received = row_swap(sent)
        across = col_swap(jnp.concatenate([own, received], axis=1))
        return own, received, across

    token_parts = split_input(tokens)
    params = jnp.stack([ln1_gain, ln1_bias, b_out, ln2_gain, ln2_bias, b_down], axis=1)
    params = jnp.concatenate([params, row_swap(params)], axis=2)
    wq = jnp.transpose(w_qkv, (0, 2, 1, 3))
    wq_oth = row_swap(wq)
    wo_oth = row_swap(w_out)
    wu_oth = row_swap(w_up)
    wd_oth = row_swap(w_down)
    cot_parts = split_input(cotangent)
    bup = b_up[:, None, :]
    info = jnp.stack(
        [
            lax.axis_index("dp"),
            col * block + row * part,
            (1 - col) * block + row * part,
            col * block + (1 - row) * part,
            (1 - col) * block + (1 - row) * part,
        ]
    ).astype(jnp.int32)
    seqs = (info, seq_lengths[None, :], seq_owner[None, :], seq_offset[None, :])
    smem = pl.BlockSpec(memory_space=pltpu.SMEM)
    head_width = w_qkv.shape[3]
    act = shape_of((rows, half), BF)
    full = shape_of((rows, width), BF)
    stream = shape_of((rows, width), F32)
    wide = shape_of((rows, hidden_part), BF)

    kept = []
    x1 = y_down = y_down_rec = None
    for l in range(LAYERS):
        outs = [stream, act, act, act, full]
        if l == 0:
            ins = [*token_parts, params, qv_bias, wq, wq_oth]
            spec = {k: layer_spec(ins[k], l) for k in (3, 4, 5, 6)}
            kernel = first_kernel
        else:
            ins = [x1, y_down, y_down_rec, params, params, qv_bias, wq, wq_oth]
            spec = {k: layer_spec(ins[k], l) for k in (4, 5, 6, 7)}
            spec[3] = layer_spec(params, l - 1)
            kernel = next_kernel
        x, a_own, a_oth, q, kv = call(kernel, ins, outs, 2 * rows * width * 3 * half, spec)
        kv_rec = row_swap(kv)
        a_rec = row_swap(a_oth)
        ins = [*seqs, q, kv, kv_rec, w_out, wo_oth]
        spec = {0: smem, 7: layer_spec(w_out, l), 8: layer_spec(wo_oth, l)}
        o, lse, y_att = call(
            attend_kernel,
            ins,
            [act, shape_of((rows, 128), F32), full],
            2 * rows * width * half * 3,
            spec,
        )
        y_att_rec = col_swap(y_att)
        o_rec = row_swap(o)
        ins = [x, y_att, y_att_rec, params, bup, w_up, wu_oth, w_down, wd_oth]
        spec = {k: layer_spec(ins[k], l) for k in range(3, 9)}
        x1, m_own, m_oth, h, gp, y_down = call(
            mlp_kernel,
            ins,
            [stream, act, act, wide, wide, full],
            4 * rows * width * hidden_part,
            spec,
        )
        m_rec = row_swap(m_oth)
        h_rec = row_swap(h)
        if l < LAYERS - 1:
            y_down_rec = col_swap(y_down)
        kept.append((x, a_own, a_rec, q, kv, kv_rec, o, o_rec, lse, x1, m_own, m_rec, h, h_rec, gp))

    y_last = col_swap(y_down[part:])
    out_rows = x1[:part] + (
        y_down[:part].astype(F32) + y_last.astype(F32) + params[LAYERS - 1, 5:6, :]
    )
    out_other = row_swap(out_rows[:, half:])
    out_own = out_rows[:, :half]

    def by_row(own, other):
        return jnp.where(
            row == 0, jnp.concatenate([own, other]), jnp.concatenate([other, own])
        )

    out_act = by_row(out_own, out_other)

    sums = [[None] * 6 for _ in range(LAYERS)]
    col_sums = [None] * LAYERS
    buffers = [None] * LAYERS
    g1 = da = da_rec = None
    for l in reversed(range(LAYERS)):
        (x, a_own, a_rec, q, kv, kv_rec, o, o_rec, lse, x1, m_own, m_rec, h, h_rec, gp) = kept[l]
        outs = [
            stream,
            act,
            act,
            wide,
            full,
            shape_of((1, width), F32),
            shape_of((1, hidden_part), F32),
        ]
        if l == LAYERS - 1:
            ins = [*cot_parts, gp, w_up, wu_oth, w_down, wd_oth]
            spec = {k: layer_spec(ins[k], l) for k in range(4, 8)}
            g, gy_own, gy_oth, du, dm, s_down, s_up = call(
                last_back_kernel, ins, outs, 4 * rows * width * hidden_part, spec
            )
        else:
            ins = [g1, da, da_rec, kept[l + 1][0], params, gp, w_up, wu_oth, w_down, wd_oth]
            spec = {k: layer_spec(ins[k], l) for k in range(6, 10)}
            spec[4] = layer_spec(params, l + 1)
            s_ln1, g, gy_own, gy_oth, du, dm, s_down, s_up = call(
                next_back_kernel,
                ins,
                [shape_of((2, width), F32)] + outs,
                4 * rows * width * hidden_part,
                spec,
            )
            sums[l + 1][0:2] = [s_ln1[0:1], s_ln1[1:2]]
        dm_rec = col_swap(dm)
        gy_rec = row_swap(gy_oth)
        du_rec = row_swap(du)
        ins = [*seqs, g, dm, dm_rec, x1, params, w_out, wo_oth, q, kv, kv_rec, lse]
        spec = {k: layer_spec(ins[k], l) for k in (8, 9, 10)}
        spec[0] = smem
        g1, ga_own, ga_oth, dq, dkv, dkv_oth, s_att = call(
            attend_back_kernel,
            ins,
            [stream, act, act, act, full, full, shape_of((3, width), F32)],
            2 * rows * width * half * 6,
            spec,
        )
        dkv_rec = row_swap(dkv_oth)
        ga_rec = row_swap(ga_oth)
        dq_rec = row_swap(dq)
        ins = [dq, dkv, dkv_rec, wq, wq_oth]
        spec = {3: layer_spec(wq, l), 4: layer_spec(wq_oth, l)}
        da, dkv_total, s_qv = call(
            project_back_kernel,
            ins,
            [full, full, shape_of((2, half), F32)],
            2 * rows * width * half * 3,
            spec,
        )
        da_rec = col_swap(da)
        dkv_total_rec = row_swap(dkv_total)
        buffers[l] = call(
            weight_grad_kernel,
            [
                h, h_rec, gy_own, gy_rec, m_own, m_rec, du, du_rec,
                o, o_rec, ga_own, ga_rec, a_own, a_rec, dq, dq_rec, dkv_total, dkv_total_rec,
            ],
            [shape_of((12 * half, half), BF)],
            2 * 2 * rows * half * half * 12,
        )[0]
        sums[l][2:6] = [s_att[0:1], s_att[1:2], s_att[2:3], s_down]
        col_sums[l] = jnp.concatenate([s_qv, s_up.reshape(-1, half)], axis=0)
    end = call(
        end_back_kernel,
        [g1, da, da_rec, kept[0][0], params],
        [shape_of((2, width), F32), shape_of((part, half), F32), shape_of((part, half), F32)],
        0,
        {4: layer_spec(params, 0)},
    )
    sums[0][0:2] = [end[0][0:1], end[0][1:2]]
    grad_tokens = by_row(end[1], row_swap(end[2]))

    totals = [data_total(buffer) for buffer in buffers]
    row_small = jnp.concatenate([piece for layer in sums for piece in layer], axis=0)
    col_small = jnp.concatenate(col_sums, axis=0)
    row_small = row_small[:, :half] + row_swap(row_small[:, half:])
    col_small = col_small + row_swap(col_small)
    small = small_total(jnp.concatenate([row_small, col_small], axis=0))
    row_small = small[: 6 * LAYERS].reshape(LAYERS, 6, half)
    col_small = small[6 * LAYERS :].reshape(LAYERS, -1, half)

    def stacked(pick):
        return jnp.stack([pick(total) for total in totals]).astype(F32)

    grad_down = stacked(lambda t: t[: 4 * half])
    grad_up = stacked(
        lambda t: jnp.concatenate([t[(4 + k) * half : (5 + k) * half] for k in range(4)], axis=1)
    )
    grad_qkv = jnp.transpose(
        stacked(lambda t: t[8 * half : 11 * half].reshape(3, half, half)), (0, 2, 1, 3)
    )
    grad_out = stacked(lambda t: t[11 * half :])
    return (
        out_act,
        grad_tokens,
        row_small[:, 0],
        row_small[:, 1],
        grad_qkv,
        col_small[:, :2],
        grad_out,
        row_small[:, 2],
        row_small[:, 3],
        row_small[:, 4],
        grad_up,
        col_small[:, 2:].reshape(LAYERS, -1),
        grad_down,
        row_small[:, 5],
    )


def solution(mesh):
    in_specs = (
        P(("dp", "col"), "row"),
        P(("dp", "col"), "row"),
        P(None, "row"),
        P(None, "row"),
        P(None, "row", None, "col"),
        P(None, None, "col"),
        P(None, "col", "row"),
        P(None, "row"),
        P(None, "row"),
        P(None, "row"),
        P(None, "row", "col"),
        P(None, "col"),
        P(None, "col", "row"),
        P(None, "row"),
        P(),
        P(),
        P(),
    )
    out_specs = (
        P(("dp", "col"), "row"),
        P(("dp", "col"), "row"),
        P(None, "row"),
        P(None, "row"),
        P(None, "row", None, "col"),
        P(None, None, "col"),
        P(None, "col", "row"),
        P(None, "row"),
        P(None, "row"),
        P(None, "row"),
        P(None, "row", "col"),
        P(None, "col"),
        P(None, "col", "row"),
        P(None, "row"),
    )
    return jax.shard_map(body, mesh=mesh, in_specs=in_specs, out_specs=out_specs, check_vma=False)
```

```python
import math
from functools import partial

import jax
import jax.numpy as jnp
from jax import lax
from jax.experimental import pallas as pl
from jax.experimental.pallas import tpu as pltpu
from jax.sharding import PartitionSpec as P

DH = 64
LAYERS = 2
EPSILON = 1e-05
MASKED_SCORE = -1e30
INV_SQRT2 = 0.7071067811865476
INV_SQRT2PI = 0.3989422804014327
BF = jnp.bfloat16
F32 = jnp.float32
VMEM_BYTES = 24 * 1024 * 1024


PARAMS = ("gain1", "bias1", "b_out", "gain2", "bias2", "b_down")


def call(kernel, ins, outs, flops=0, specs=None, after=(), aliases=None):
    count = len(ins)

    def run(*refs):
        kernel(*refs[:count], *refs[count + len(after) :])

    in_specs = []
    for position, operand in enumerate(ins):
        spec = (specs or {}).get(position)
        in_specs.append(spec if spec is not None else whole_spec(operand))
    in_specs += [pl.BlockSpec(memory_space=pl.ANY)] * len(after)
    out_specs = [x[1] if isinstance(x, tuple) else whole_spec(x) for x in outs]
    outs = [x[0] if isinstance(x, tuple) else x for x in outs]
    size = sum(math.prod(x.shape) * x.dtype.itemsize for x in (*ins, *outs))
    return pl.pallas_call(
        run,
        out_shape=outs,
        in_specs=in_specs,
        out_specs=out_specs,
        grid=(1,),
        input_output_aliases=aliases or {},
        compiler_params=pltpu.CompilerParams(vmem_limit_bytes=VMEM_BYTES),
        cost_estimate=pl.CostEstimate(flops=flops, bytes_accessed=size, transcendentals=0),
    )(*ins, *after)


def whole_spec(operand):
    zeros = (0,) * len(operand.shape)
    return pl.BlockSpec(operand.shape, lambda i: zeros)


def layer_spec(operand, layer):
    rest = operand.shape[1:]
    zeros = (0,) * len(rest)
    return pl.BlockSpec((None,) + rest, lambda i: (layer,) + zeros)


def shape_of(shape, dtype):
    return jax.ShapeDtypeStruct(shape, dtype)


def kept_of(shape, dtype):
    return pltpu.HBM(shape, dtype)


def mm(left, right):
    return jnp.dot(left, right, preferred_element_type=F32)


def mm_nt(left, right):
    return lax.dot_general(left, right, (((1,), (1,)), ((), ())), preferred_element_type=F32)


def mm_tn(left, right):
    return lax.dot_general(left, right, (((0,), (0,)), ((), ())), preferred_element_type=F32)


def swapped(ref):
    half = ref.shape[0] // 2
    return jnp.concatenate([ref[half:, :], ref[:half, :]], axis=0).astype(F32)


def both(own_ref, received_ref):
    return own_ref[...].astype(F32) + swapped(received_ref)


def statistics(inputs):
    center = jnp.mean(inputs, axis=1, keepdims=True)
    second = jnp.mean(inputs * inputs, axis=1, keepdims=True)
    inverse = lax.rsqrt(second - center * center + EPSILON)
    return (inputs - center) * inverse, inverse


def norm_grad(grad_norm, normal, inverse, gain):
    scaled = grad_norm * gain
    first = jnp.mean(scaled, axis=1, keepdims=True)
    second = jnp.mean(scaled * normal, axis=1, keepdims=True)
    return inverse * (scaled - first - normal * second)


def col_sum(values):
    return jnp.sum(values.astype(F32), axis=0, keepdims=True)


def pieces(own_ref, row_ref, col_ref):
    mine = jnp.concatenate([own_ref[...], row_ref[...]], axis=1)
    return jnp.concatenate([mine, col_ref[...]], axis=0).astype(F32)


def qkv_part(hidden, gain, bias, w_own, w_oth, qvb_ref, x_ref, a_own, a_oth, q_ref, kv_ref):
    x_ref[...] = hidden
    normal, _ = statistics(hidden)
    normed = (normal * gain + bias).astype(BF)
    half = normed.shape[1] // 2
    left, right = normed[:, :half], normed[:, half:]
    a_own[...] = left
    a_oth[...] = right
    width = q_ref.shape[1]
    q_ref[...] = (mm(left, w_own[0]) + mm(right, w_oth[0]) + qvb_ref[0:1, :]).astype(BF)
    kv_ref[:, :width] = (mm(left, w_own[1]) + mm(right, w_oth[1])).astype(BF)
    kv_ref[:, width:] = (mm(left, w_own[2]) + mm(right, w_oth[2]) + qvb_ref[1:2, :]).astype(BF)


def param(par, name, layer):
    at = PARAMS.index(name) * LAYERS + layer
    return par[at : at + 1, :]


def first_kernel(layer, own, row, col, par, qvb, w_own, w_oth, *outs):
    hidden = pieces(own, row, col)
    qkv_part(
        hidden, param(par, "gain1", layer), param(par, "bias1", layer), w_own, w_oth, qvb, *outs
    )


def next_kernel(layer, x1, y_own, y_rec, par, qvb, w_own, w_oth, *outs):
    hidden = x1[...] + (both(y_own, y_rec) + param(par, "b_down", layer - 1))
    qkv_part(
        hidden, param(par, "gain1", layer), param(par, "bias1", layer), w_own, w_oth, qvb, *outs
    )


def attention_mask(info, seq_len, seq_own, seq_off, rows, cols):
    quarter = rows // 2
    i = lax.broadcasted_iota(jnp.int32, (rows, 1), 0)
    j = lax.broadcasted_iota(jnp.int32, (1, cols), 1)
    pos_q = jnp.where(i < quarter, info[1] + i, info[2] + i - quarter)
    pos_k = jnp.where(
        j < 2 * quarter,
        jnp.where(j < quarter, info[1] + j, info[2] + j - quarter),
        jnp.where(j < 3 * quarter, info[3] + j - 2 * quarter, info[4] + j - 3 * quarter),
    )
    offset = seq_off[...]
    inside = (
        (seq_own[...] == info[0]) & (pos_q >= offset) & (pos_q < offset + seq_len[...])
    )
    start = jnp.max(jnp.where(inside, offset, -1), axis=1, keepdims=True)
    start = jnp.where(start < 0, pos_q, start)
    return (pos_k <= pos_q) & (pos_k >= start)


def head_lanes(rows, which):
    lane = lax.broadcasted_iota(jnp.int32, (rows, 2 * DH), 1)
    return (lane < DH) if which == 0 else (lane >= DH)


def attend_kernel(
    info, seq_len, seq_own, seq_off, q, kv_own, kv_oth, o_ref, lse_ref
):
    rows, width = q.shape
    mask = attention_mask(info, seq_len, seq_own, seq_off, rows, 2 * rows)
    sides = [head_lanes(rows, 0), head_lanes(rows, 1)]
    lane = lax.broadcasted_iota(jnp.int32, (rows, 128), 1)
    logs = jnp.zeros((rows, 128), F32)
    scale = DH**-0.5
    for pair in range(width // (2 * DH)):
        span = slice(pair * 2 * DH, (pair + 1) * 2 * DH)
        vspan = slice(width + pair * 2 * DH, width + (pair + 1) * 2 * DH)
        queries = q[:, span] * jnp.asarray(scale, BF)
        keys = jnp.concatenate([kv_own[:, span], kv_oth[:, span]], axis=0)
        values = jnp.concatenate([kv_own[:, vspan], kv_oth[:, vspan]], axis=0)
        mixed = None
        for side in range(2):
            scores = mm_nt(jnp.where(sides[side], queries, jnp.zeros_like(queries)), keys)
            scores = jnp.where(mask, scores, MASKED_SCORE)
            largest = jnp.max(scores, axis=1, keepdims=True)
            powers = jnp.exp(scores - largest)
            total = jnp.sum(powers, axis=1, keepdims=True)
            out = mm((powers * (1.0 / total)).astype(BF), values)
            logs = jnp.where(lane == 2 * pair + side, largest + jnp.log(total), logs)
            mixed = out if side == 0 else jnp.where(sides[0], mixed, out)
        o_ref[:, span] = mixed.astype(BF)
    lse_ref[...] = logs


def mlp_kernel(
    layer, x, o_own, o_rec, par, wo_own, wo_oth, wc_own, wc_oth,
    bup, wu_own, wu_oth, wd_own, wd_oth,
    x1_ref, m_own, m_oth, h_ref, gp_ref, y_ref,
):
    mixed = o_own[...]
    quarter = o_rec.shape[0] // 2
    mixed_other = jnp.concatenate([o_rec[quarter:, :], o_rec[:quarter, :]], axis=0)
    attended = jnp.concatenate(
        [
            mm(mixed, wo_own[...]) + mm(mixed_other, wc_own[...]),
            mm(mixed, wo_oth[...]) + mm(mixed_other, wc_oth[...]),
        ],
        axis=1,
    )
    middle = x[...] + (attended + param(par, "b_out", layer))
    x1_ref[...] = middle
    normal, _ = statistics(middle)
    normed = (normal * param(par, "gain2", layer) + param(par, "bias2", layer)).astype(BF)
    half = normed.shape[1] // 2
    left, right = normed[:, :half], normed[:, half:]
    m_own[...] = left
    m_oth[...] = right
    width = h_ref.shape[1]
    step = 384
    out_own = out_oth = None
    for at in range(0, width, step):
        span = slice(at, at + step)
        upward = mm(left, wu_own[:, span]) + mm(right, wu_oth[:, span]) + bup[:, span]
        phi = 0.5 + 0.5 * lax.erf(upward * INV_SQRT2)
        density = jnp.exp(-0.5 * upward * upward) * INV_SQRT2PI
        active = (upward * phi).astype(BF)
        h_ref[:, span] = active
        gp_ref[:, span] = (phi + upward * density).astype(BF)
        part_own = mm(active, wd_own[span, :])
        part_oth = mm(active, wd_oth[span, :])
        out_own = part_own if out_own is None else out_own + part_own
        out_oth = part_oth if out_oth is None else out_oth + part_oth
    y_ref[:, :half] = out_own.astype(BF)
    y_ref[:, half:] = out_oth.astype(BF)


def mlp_back(
    grad, gp, wu_own, wu_oth, wd_own, wd_oth,
    g_ref, gy_own, gy_oth, du_ref, dm_ref, sdown_ref, sup_ref,
):
    g_ref[...] = grad
    branch = grad.astype(BF)
    half = branch.shape[1] // 2
    left, right = branch[:, :half], branch[:, half:]
    gy_own[...] = left
    gy_oth[...] = right
    sdown_ref[...] = col_sum(branch)
    width = gp.shape[1]
    step = 384
    out_own = out_oth = None
    for at in range(0, width, step):
        span = slice(at, at + step)
        grad_active = mm_nt(left, wd_own[span, :]) + mm_nt(right, wd_oth[span, :])
        grad_up = (grad_active * gp[:, span].astype(F32)).astype(BF)
        du_ref[:, span] = grad_up
        sup_ref[at // step : at // step + 1, :] = col_sum(grad_up)
        part_own = mm_nt(grad_up, wu_own[:, span])
        part_oth = mm_nt(grad_up, wu_oth[:, span])
        out_own = part_own if out_own is None else out_own + part_own
        out_oth = part_oth if out_oth is None else out_oth + part_oth
    dm_ref[:, :half] = out_own.astype(BF)
    dm_ref[:, half:] = out_oth.astype(BF)


def last_back_kernel(own, row, col, gp, wu_own, wu_oth, wd_own, wd_oth, *outs):
    mlp_back(pieces(own, row, col), gp, wu_own, wu_oth, wd_own, wd_oth, *outs)


def input_grad(layer, g1, da_own, da_rec, x, par, small_ref):
    grad_normed = both(da_own, da_rec)
    normal, inverse = statistics(x[...])
    small_ref[0:1, :] = col_sum(grad_normed * normal)
    small_ref[1:2, :] = col_sum(grad_normed)
    return g1[...] + norm_grad(
        grad_normed, normal, inverse, param(par, "gain1", layer)
    )


def next_back_kernel(
    layer, g1, da_own, da_rec, x, par, gp, wu_own, wu_oth, wd_own, wd_oth, small_ref, *outs
):
    grad = input_grad(layer + 1, g1, da_own, da_rec, x, par, small_ref)
    mlp_back(grad, gp, wu_own, wu_oth, wd_own, wd_oth, *outs)


def end_back_kernel(layer, g1, da_own, da_rec, x, par, small_ref, own_ref, oth_ref):
    grad = input_grad(layer, g1, da_own, da_rec, x, par, small_ref)
    rows, width = grad.shape
    own_ref[...] = grad[: rows // 2, : width // 2]
    oth_ref[...] = grad[: rows // 2, width // 2 :]


def attend_back_kernel(
    layer, info, seq_len, seq_own, seq_off, grad, dm_own, dm_rec, x1, par, w_own, w_oth,
    q, kv_own, kv_oth, lse,
    g1_ref, ga_own, ga_oth, dq_ref, dkv_own, dkv_oth, small_ref,
):
    grad_normed = both(dm_own, dm_rec)
    normal, inverse = statistics(x1[...])
    grad_middle = grad[...] + norm_grad(
        grad_normed, normal, inverse, param(par, "gain2", layer)
    )
    g1_ref[...] = grad_middle
    branch = grad_middle.astype(BF)
    small_ref[0:1, :] = col_sum(branch)
    small_ref[1:2, :] = col_sum(grad_normed * normal)
    small_ref[2:3, :] = col_sum(grad_normed)
    half = branch.shape[1] // 2
    left, right = branch[:, :half], branch[:, half:]
    ga_own[...] = left
    ga_oth[...] = right
    grad_mixed = (mm_nt(left, w_own[...]) + mm_nt(right, w_oth[...])).astype(BF)
    rows, width = q.shape
    mask = attention_mask(info, seq_len, seq_own, seq_off, rows, 2 * rows)
    sides = [head_lanes(rows, 0), head_lanes(rows, 1)]
    key_sides = head_lanes(2 * rows, 0)
    scale = DH**-0.5
    for pair in range(width // (2 * DH)):
        span = slice(pair * 2 * DH, (pair + 1) * 2 * DH)
        vspan = slice(width + pair * 2 * DH, width + (pair + 1) * 2 * DH)
        queries = q[:, span] * jnp.asarray(scale, BF)
        keys = jnp.concatenate([kv_own[:, span], kv_oth[:, span]], axis=0)
        values = jnp.concatenate([kv_own[:, vspan], kv_oth[:, vspan]], axis=0)
        grad_out = grad_mixed[:, span]
        grad_q = grad_k = grad_v = None
        for side in range(2):
            head = 2 * pair + side
            scores = mm_nt(jnp.where(sides[side], queries, jnp.zeros_like(queries)), keys)
            scores = jnp.where(mask, scores, MASKED_SCORE)
            probability = jnp.exp(scores - lse[:, head : head + 1])
            grad_prob = mm_nt(jnp.where(sides[side], grad_out, jnp.zeros_like(grad_out)), values)
            inner = jnp.sum(grad_prob * probability, axis=1, keepdims=True)
            grad_scores = (probability * (grad_prob - inner)).astype(BF)
            part_q = mm(grad_scores, keys)
            part_k = mm_tn(grad_scores, queries)
            part_v = mm_tn(probability.astype(BF), grad_out)
            if side == 0:
                grad_q, grad_k, grad_v = part_q, part_k, part_v
            else:
                grad_q = jnp.where(sides[0], grad_q, part_q)
                grad_k = jnp.where(key_sides, grad_k, part_k)
                grad_v = jnp.where(key_sides, grad_v, part_v)
        dq_ref[:, span] = (grad_q * scale).astype(BF)
        dkv_own[:, span] = grad_k[:rows].astype(dkv_own.dtype)
        dkv_oth[:, span] = grad_k[rows:].astype(dkv_oth.dtype)
        dkv_own[:, vspan] = grad_v[:rows].astype(dkv_own.dtype)
        dkv_oth[:, vspan] = grad_v[rows:].astype(dkv_oth.dtype)


def project_back_kernel(dq, dkv_own, dkv_rec, w_own, w_oth, da_ref, dkv_ref, small_ref):
    width = dq.shape[1]
    total = (dkv_own[...].astype(F32) + dkv_rec[...].astype(F32)).astype(BF)
    dkv_ref[...] = total
    small_ref[0:1, :] = col_sum(dq[...])
    small_ref[1:2, :] = col_sum(total[:, width:])
    parts = (dq[...], total[:, :width], total[:, width:])
    half = da_ref.shape[1] // 2
    for at, weight in ((0, w_own), (half, w_oth)):
        out = mm_nt(parts[0], weight[0]) + mm_nt(parts[1], weight[1]) + mm_nt(parts[2], weight[2])
        da_ref[:, at : at + half] = out.astype(BF)


def grad_term(left_own, left_rec, right_own, right_rec):
    return (mm_tn(left_own, right_own) + mm_tn(left_rec, right_rec)).astype(BF)


def mlp_grads(h_own, h_rec, gy_own, gy_rec, m_own, m_rec, du_own, du_rec, out_ref):
    size = gy_own.shape[1]
    for k in range(h_own.shape[1] // size):
        span = slice(k * size, (k + 1) * size)
        out_ref[span, :] = grad_term(h_own[:, span], h_rec[:, span], gy_own[...], gy_rec[...])
    base = h_own.shape[1]
    for k in range(du_own.shape[1] // size):
        span = slice(k * size, (k + 1) * size)
        out_ref[base + k * size : base + (k + 1) * size, :] = grad_term(
            m_own[...], m_rec[...], du_own[:, span], du_rec[:, span]
        )


def attention_grads(
    o_own, o_rec, ga_own, ga_rec, a_own, a_rec, dq_own, dq_rec, dkv_own, dkv_rec, out_ref, base=0
):
    size = ga_own.shape[1]
    spans = [slice(base + k * size, base + (k + 1) * size) for k in range(4)]
    out_ref[spans[0], :] = grad_term(a_own[...], a_rec[...], dq_own[...], dq_rec[...])
    for k in range(2):
        span = slice(k * size, (k + 1) * size)
        out_ref[spans[1 + k], :] = grad_term(
            a_own[...], a_rec[...], dkv_own[:, span], dkv_rec[:, span]
        )
    out_ref[spans[3], :] = grad_term(o_own[...], o_rec[...], ga_own[...], ga_rec[...])


def joined(side, own, other):
    first = side[0] == 0
    return jnp.where(first, own[...], other[...]), jnp.where(first, other[...], own[...])


def mlp_result_kernel(side, own, other, *refs):
    up_ref, down_ref = refs[-2:]
    down, up = joined(side, own, other)
    down_ref[...] = down.astype(F32)
    size = down_ref.shape[1]
    for k in range(up_ref.shape[1] // size):
        span = slice(k * size, (k + 1) * size)
        up_ref[:, span] = up[span, :].astype(F32)


def attention_result_kernel(side, own, other, *refs):
    qkv_ref, out_ref = refs[-2:]
    size = out_ref.shape[1]
    low, high = joined(side, own, other)
    qkv_ref[0] = low[:size].astype(F32)
    qkv_ref[1] = low[size:].astype(F32)
    qkv_ref[2] = high[:size].astype(F32)
    out_ref[...] = high[size:].astype(F32)


SWAP = [(0, 1), (1, 0)]


def row_swap(operand):
    return lax.ppermute(operand, "row", SWAP)


def col_swap(operand):
    return lax.ppermute(operand, "col", SWAP)


def flipped(index, pairing):
    z, x, y = index // 8, (index // 2) % 4, index % 2
    if pairing == "za":
        z ^= 1
    elif pairing == "zb":
        z = 3 - z
    elif pairing == "xa":
        x ^= 1
    elif pairing == "xb":
        x = 3 - x
    else:
        y ^= 1
    return z * 8 + x * 2 + y


def side_of(index, pairing):
    z, x, y = index // 8, (index // 2) % 4, index % 2
    return {
        "za": (z + 1) // 2 % 2,
        "zb": z // 2,
        "xa": (x + 1) // 2 % 2,
        "xb": x // 2,
        "y": y,
    }[pairing]


def exchange(operand, pairings):
    table = [
        (dp * 2 + row, flipped(dp, pairings[row]) * 2 + row) for dp in range(32) for row in range(2)
    ]
    return lax.ppermute(operand, ("dp", "row"), table)


def my_side(pairings):
    dp = lax.axis_index("dp")
    return jnp.where(
        lax.axis_index("row") == 0, side_of(dp, pairings[0]), side_of(dp, pairings[1])
    )


def halve(operand, pairings):
    half = operand.shape[0] // 2
    side = my_side(pairings)
    sent = lax.dynamic_slice_in_dim(operand, (1 - side) * half, half, 0)
    received = exchange(sent, pairings)
    kept = lax.dynamic_slice_in_dim(operand, side * half, half, 0)
    return (kept.astype(F32) + received.astype(F32)).astype(BF)


def double(operand, pairings):
    other = exchange(operand, pairings)
    return jnp.where(
        my_side(pairings) == 0,
        jnp.concatenate([operand, other]),
        jnp.concatenate([other, operand]),
    )


Z_FIRST = [("za", "xa"), ("xa", "za"), ("zb", "xb"), ("xb", "zb"), ("y", "y")]
B_FIRST = [("zb", "xb"), ("xb", "zb"), ("za", "xa"), ("xa", "za"), ("y", "y")]


class DataTotal:
    def __init__(self, operand, order, halvings):
        self.value, self.order, self.halvings, self.done = operand, order, halvings, 0

    def step(self):
        count = len(self.order)
        if self.done < self.halvings:
            self.value = halve(self.value, self.order[self.done])
        elif self.done < count:
            received = exchange(self.value, self.order[self.done])
            self.value = (self.value.astype(F32) + received.astype(F32)).astype(BF)
        else:
            self.value = double(self.value, self.order[count + self.halvings - 1 - self.done])
        self.done += 1
        return self.value

    def last(self):
        while self.done < len(self.order) + self.halvings - 1:
            self.step()
        pairings = self.order[0]
        side = my_side(pairings).astype(jnp.int32).reshape(1)
        return side, self.value, exchange(self.value, pairings)


def small_total(operand):
    for pairing in ("za", "xa", "zb", "xb", "y"):
        operand = operand + exchange(operand, (pairing, pairing))
    return operand


def body(
    tokens,
    cotangent,
    ln1_gain,
    ln1_bias,
    w_qkv,
    qv_bias,
    w_out,
    b_out,
    ln2_gain,
    ln2_bias,
    w_up,
    b_up,
    w_down,
    b_down,
    seq_lengths,
    seq_owner,
    seq_offset,
):
    row = lax.axis_index("row")
    col = lax.axis_index("col")
    block, half = tokens.shape
    part = block // 2
    rows = block
    width = 2 * half
    hidden_part = w_up.shape[2]

    def split_input(operand):
        own = lax.dynamic_slice_in_dim(operand, row * part, part, 0)
        sent = lax.dynamic_slice_in_dim(operand, (1 - row) * part, part, 0)
        received = row_swap(sent)
        across = col_swap(jnp.concatenate([own, received], axis=1))
        return own, received, across

    token_parts = split_input(tokens)
    params = jnp.concatenate([ln1_gain, ln1_bias, b_out, ln2_gain, ln2_bias, b_down], axis=0)
    params = jnp.concatenate([params, row_swap(params)], axis=1)
    wq = jnp.transpose(w_qkv, (0, 2, 1, 3))
    wq_oth = row_swap(wq)
    wo_oth = row_swap(w_out)
    wu_oth = row_swap(w_up)
    wd_oth = row_swap(w_down)
    wc_own = col_swap(w_out)
    wc_oth = row_swap(wc_own)
    cot_parts = split_input(cotangent)
    bup = b_up[:, None, :]
    info = jnp.stack(
        [
            lax.axis_index("dp"),
            col * block + row * part,
            (1 - col) * block + row * part,
            col * block + (1 - row) * part,
            (1 - col) * block + (1 - row) * part,
        ]
    ).astype(jnp.int32)
    seqs = (info, seq_lengths[None, :], seq_owner[None, :], seq_offset[None, :])
    smem = pl.BlockSpec(memory_space=pltpu.SMEM)
    head_width = w_qkv.shape[3]
    act = shape_of((rows, half), BF)
    full = shape_of((rows, width), BF)
    act_kept = kept_of((rows, half), BF)
    stream_kept = kept_of((rows, width), F32)
    wide_kept = kept_of((rows, hidden_part), BF)

    kept = []
    x1 = y_down = y_down_rec = None
    for l in range(LAYERS):
        outs = [stream_kept, act_kept, act_kept, act_kept, full]
        if l == 0:
            ins = [*token_parts, params, qv_bias, wq, wq_oth]
            kernel = partial(first_kernel, l)
        else:
            ins = [x1, y_down, y_down_rec, params, qv_bias, wq, wq_oth]
            kernel = partial(next_kernel, l)
        spec = {k: layer_spec(ins[k], l) for k in (4, 5, 6)}
        x, a_own, a_oth, q, kv = call(kernel, ins, outs, 2 * rows * width * 3 * half, spec)
        kv_rec = row_swap(kv)
        a_rec = row_swap(a_oth)
        ins = [*seqs, q, kv, kv_rec]
        o, lse = call(
            attend_kernel,
            ins,
            [act, kept_of((rows, 128), F32)],
            2 * rows * width * half * 2,
            {0: smem},
        )
        o_across = col_swap(o)
        o_rec = row_swap(o)
        ins = [x, o, o_across, params, w_out, wo_oth, wc_own, wc_oth]
        ins += [bup, w_up, wu_oth, w_down, wd_oth]
        spec = {k: layer_spec(ins[k], l) for k in range(4, 13)}
        x1, m_own, m_oth, h, gp, y_down = call(
            partial(mlp_kernel, l),
            ins,
            [stream_kept, act_kept, act_kept, wide_kept, wide_kept, full],
            4 * rows * width * hidden_part,
            spec,
        )
        m_rec = row_swap(m_oth)
        h_rec = row_swap(h)
        if l < LAYERS - 1:
            y_down_rec = col_swap(y_down)
        kept.append((x, a_own, a_rec, q, kv, kv_rec, o, o_rec, lse, x1, m_own, m_rec, h, h_rec, gp))

    y_last = col_swap(y_down[part:])
    out_rows = x1[:part] + (
        y_down[:part].astype(F32) + y_last.astype(F32) + params[-1:, :]
    )
    out_other = row_swap(out_rows[:, half:])
    out_own = out_rows[:, :half]

    def by_row(own, other):
        return jnp.where(
            row == 0, jnp.concatenate([own, other]), jnp.concatenate([other, own])
        )

    out_act = by_row(out_own, out_other)

    sums = [[None] * 6 for _ in range(LAYERS)]
    col_sums = [None] * LAYERS
    flops = rows * width * half

    def mlp_total(layer, gy_own, gy_rec, du, du_rec, order, halvings):
        h, h_rec, m_own, m_rec = kept[layer][12], kept[layer][13], kept[layer][10], kept[layer][11]
        grads = call(
            mlp_grads,
            [h, h_rec, gy_own, gy_rec, m_own, m_rec, du, du_rec],
            [shape_of((8 * half, half), BF)],
            4 * rows * half * half * 8,
        )[0]
        return grads, DataTotal(grads, order, halvings)

    def attention_total(layer, ga_own, ga_rec, dq, dq_rec, dkv, dkv_rec, order, halvings):
        a_own, a_rec, o, o_rec = kept[layer][1], kept[layer][2], kept[layer][6], kept[layer][7]
        grads = call(
            attention_grads,
            [o, o_rec, ga_own, ga_rec, a_own, a_rec, dq, dq_rec, dkv, dkv_rec],
            [shape_of((4 * half, half), BF)],
            4 * rows * half * half * 4,
        )[0]
        return grads, DataTotal(grads, order, halvings)

    def mlp_stage(layer, kernel, ins, outs, after):
        first = len(ins)
        ins = ins + [kept[layer][14], w_up, wu_oth, w_down, wd_oth]
        spec = {k: layer_spec(ins[k], layer) for k in range(first + 1, first + 5)}
        return call(kernel, ins, outs, 4 * flops * 4, spec, after)

    def attend_stage(layer, g, dm, dm_rec, after):
        x1, q, kv, kv_rec, lse = (kept[layer][k] for k in (9, 3, 4, 5, 8))
        ins = [*seqs, g, dm, dm_rec, x1, params, w_out, wo_oth, q, kv, kv_rec, lse]
        spec = {0: smem, 9: layer_spec(w_out, layer), 10: layer_spec(wo_oth, layer)}
        return call(
            partial(attend_back_kernel, layer),
            ins,
            [stream_kept, act_kept, act_kept, act, full, full, shape_of((3, width), F32)],
            6 * flops,
            spec,
            after,
        )

    def project_stage(layer, dq, dkv, dkv_rec):
        ins = [dq, dkv, dkv_rec, wq, wq_oth]
        spec = {3: layer_spec(wq, layer), 4: layer_spec(wq_oth, layer)}
        return call(
            project_back_kernel, ins, [full, full, shape_of((2, half), F32)], 6 * flops, spec
        )

    outs = [
        stream_kept,
        act_kept,
        act_kept,
        wide_kept,
        full,
        shape_of((1, width), F32),
        shape_of((hidden_part // half, half), F32),
    ]
    g, gy_own, gy_oth, du, dm, s_down, s_up = mlp_stage(
        1, last_back_kernel, list(cot_parts), outs, ()
    )
    dm_rec, gy_rec, du_rec = col_swap(dm), row_swap(gy_oth), row_swap(du)
    made, mlp_one = mlp_total(1, gy_own, gy_rec, du, du_rec, Z_FIRST, 3)
    g1, ga_own, ga_oth, dq, dkv, dkv_oth, s_att = attend_stage(1, g, dm, dm_rec, (made,))
    dkv_rec, ga_rec, dq_rec = row_swap(dkv_oth), row_swap(ga_oth), row_swap(dq)
    da, dkv_total, s_qv = project_stage(1, dq, dkv, dkv_rec)
    da_rec, dkv_total_rec = col_swap(da), row_swap(dkv_total)
    made, attention_one = attention_total(
        1, ga_own, ga_rec, dq, dq_rec, dkv_total, dkv_total_rec, B_FIRST, 2
    )
    sums[1][2:6] = [s_att[0:1], s_att[1:2], s_att[2:3], s_down]
    col_sums[1] = jnp.concatenate([s_qv, s_up], axis=0)
    after = (made, mlp_one.step())
    s_ln1, g, gy_own, gy_oth, du, dm, s_down, s_up = mlp_stage(
        0,
        partial(next_back_kernel, 0),
        [g1, da, da_rec, kept[1][0], params],
        [shape_of((2, width), F32)] + outs,
        after,
    )
    sums[1][0:2] = [s_ln1[0:1], s_ln1[1:2]]
    dm_rec, gy_rec, du_rec = col_swap(dm), row_swap(gy_oth), row_swap(du)
    made, mlp_zero = mlp_total(0, gy_own, gy_rec, du, du_rec, B_FIRST, 3)
    after = (made, mlp_one.step(), attention_one.step())
    g1, ga_own, ga_oth, dq, dkv, dkv_oth, s_att = attend_stage(0, g, dm, dm_rec, after)
    dkv_rec, ga_rec, dq_rec = row_swap(dkv_oth), row_swap(ga_oth), row_swap(dq)
    da, dkv_total, s_qv = project_stage(0, dq, dkv, dkv_rec)
    da_rec, dkv_total_rec = col_swap(da), row_swap(dkv_total)
    made, attention_zero = attention_total(
        0, ga_own, ga_rec, dq, dq_rec, dkv_total, dkv_total_rec, Z_FIRST, 2
    )
    sums[0][2:6] = [s_att[0:1], s_att[1:2], s_att[2:3], s_down]
    col_sums[0] = jnp.concatenate([s_qv, s_up], axis=0)
    after = (made, mlp_one.step(), attention_one.step(), mlp_zero.step())
    end = call(
        partial(end_back_kernel, 0),
        [g1, da, da_rec, kept[0][0], params],
        [shape_of((2, width), F32), shape_of((part, half), F32), shape_of((part, half), F32)],
        after=after,
    )
    sums[0][0:2] = [end[0][0:1], end[0][1:2]]
    grad_tokens = by_row(end[1], row_swap(end[2]))

    def result(kernel, total, layer, shapes, before):
        ins = [*total.last(), *before]
        specs = {0: smem}
        for k in range(3, len(ins)):
            specs[k] = pl.BlockSpec(memory_space=pl.ANY)
        aliases = {3 + k: k for k in range(len(before))}
        outs = [(shape, layer_spec(shape, layer)) for shape in shapes]
        return call(kernel, ins, outs, 0, specs, aliases=aliases)

    mlp_shapes = [shape_of(w_up.shape, F32), shape_of(w_down.shape, F32)]
    attention_shapes = [shape_of(wq.shape, F32), shape_of(w_out.shape, F32)]
    before = result(mlp_result_kernel, mlp_one, 1, mlp_shapes, [])
    grad_up, grad_down = result(mlp_result_kernel, mlp_zero, 0, mlp_shapes, before)
    before = result(attention_result_kernel, attention_one, 1, attention_shapes, [])
    grad_qkv, grad_out = result(
        attention_result_kernel, attention_zero, 0, attention_shapes, before
    )
    grad_qkv = jnp.transpose(grad_qkv, (0, 2, 1, 3))

    row_small = jnp.concatenate([piece for layer in sums for piece in layer], axis=0)
    col_small = jnp.concatenate(col_sums, axis=0)
    row_small = row_small[:, :half] + row_swap(row_small[:, half:])
    col_small = col_small + row_swap(col_small)
    small = small_total(jnp.concatenate([row_small, col_small], axis=0))
    row_small = small[: 6 * LAYERS].reshape(LAYERS, 6, half)
    col_small = small[6 * LAYERS :].reshape(LAYERS, -1, half)

    return (
        out_act,
        grad_tokens,
        row_small[:, 0],
        row_small[:, 1],
        grad_qkv,
        col_small[:, :2],
        grad_out,
        row_small[:, 2],
        row_small[:, 3],
        row_small[:, 4],
        grad_up,
        col_small[:, 2:].reshape(LAYERS, -1),
        grad_down,
        row_small[:, 5],
    )


def solution(mesh):
    in_specs = (
        P(("dp", "col"), "row"),
        P(("dp", "col"), "row"),
        P(None, "row"),
        P(None, "row"),
        P(None, "row", None, "col"),
        P(None, None, "col"),
        P(None, "col", "row"),
        P(None, "row"),
        P(None, "row"),
        P(None, "row"),
        P(None, "row", "col"),
        P(None, "col"),
        P(None, "col", "row"),
        P(None, "row"),
        P(),
        P(),
        P(),
    )
    out_specs = (
        P(("dp", "col"), "row"),
        P(("dp", "col"), "row"),
        P(None, "row"),
        P(None, "row"),
        P(None, "row", None, "col"),
        P(None, None, "col"),
        P(None, "col", "row"),
        P(None, "row"),
        P(None, "row"),
        P(None, "row"),
        P(None, "row", "col"),
        P(None, "col"),
        P(None, "col", "row"),
        P(None, "row"),
    )
    return jax.shard_map(body, mesh=mesh, in_specs=in_specs, out_specs=out_specs, check_vma=False)
```

```python
import math
from functools import partial

import jax
import jax.numpy as jnp
from jax import lax
from jax.experimental import pallas as pl
from jax.experimental.pallas import tpu as pltpu
from jax.sharding import PartitionSpec as P

DH = 64
LAYERS = 2
EPSILON = 1e-05
MASKED_SCORE = -1e30
INV_SQRT2 = 0.7071067811865476
INV_SQRT2PI = 0.3989422804014327
BF = jnp.bfloat16
F32 = jnp.float32
VMEM_BYTES = 32 * 1024 * 1024
VMEM_EXTRA = 4 * 1024 * 1024


SMALL_ROWS = 64
PARAMS = ("gain1", "bias1", "b_out", "gain2", "bias2", "b_down")


def call(kernel, ins, outs, flops=0, specs=None, after=(), aliases=None, scratch=()):
    count = len(ins)

    def run(*refs):
        kernel(*refs[:count], *refs[count + len(after) :])

    in_specs = []
    placed = []
    for position, operand in enumerate(ins):
        spec = (specs or {}).get(position)
        in_specs.append(spec if spec is not None else whole_spec(operand))
        placed.append(operand)
    in_specs += [pl.BlockSpec(memory_space=pl.ANY)] * len(after)
    out_specs = [x[1] if isinstance(x, tuple) else whole_spec(x) for x in outs]
    outs = [x[0] if isinstance(x, tuple) else x for x in outs]
    size = sum(math.prod(x.shape) * x.dtype.itemsize for x in (*ins, *outs))
    return pl.pallas_call(
        run,
        out_shape=outs,
        in_specs=in_specs,
        out_specs=out_specs,
        grid=(1,),
        input_output_aliases=aliases or {},
        scratch_shapes=list(scratch),
        compiler_params=pltpu.CompilerParams(vmem_limit_bytes=min(VMEM_BYTES, size + size // 2 + VMEM_EXTRA)),
        cost_estimate=pl.CostEstimate(flops=flops, bytes_accessed=size, transcendentals=0),
    )(*placed, *after)


def whole_spec(operand):
    zeros = (0,) * len(operand.shape)
    return pl.BlockSpec(operand.shape, lambda i: zeros)


def layer_spec(operand, layer):
    rest = operand.shape[1:]
    zeros = (0,) * len(rest)
    return pl.BlockSpec((None,) + rest, lambda i: (layer,) + zeros)


def shape_of(shape, dtype):
    return jax.ShapeDtypeStruct(shape, dtype)


def kept_of(shape, dtype):
    return jax.ShapeDtypeStruct(shape, dtype)


def mm(left, right):
    return jnp.dot(left, right, preferred_element_type=F32)


def mm_nt(left, right):
    return lax.dot_general(left, right, (((1,), (1,)), ((), ())), preferred_element_type=F32)


def mm_tn(left, right):
    return lax.dot_general(left, right, (((0,), (0,)), ((), ())), preferred_element_type=F32)


def swapped(ref):
    half = ref.shape[0] // 2
    return jnp.concatenate([ref[half:, :], ref[:half, :]], axis=0).astype(F32)


def both(own_ref, received_ref):
    return own_ref[...].astype(F32) + swapped(received_ref)


def statistics(inputs):
    center = jnp.mean(inputs, axis=1, keepdims=True)
    second = jnp.mean(inputs * inputs, axis=1, keepdims=True)
    inverse = lax.rsqrt(second - center * center + EPSILON)
    return (inputs - center) * inverse, inverse


def norm_grad(grad_norm, normal, inverse, gain):
    scaled = grad_norm * gain
    first = jnp.mean(scaled, axis=1, keepdims=True)
    second = jnp.mean(scaled * normal, axis=1, keepdims=True)
    return inverse * (scaled - first - normal * second)


def col_sum(values):
    return jnp.sum(values.astype(F32), axis=0, keepdims=True)


def pieces(own_ref, row_ref, col_ref):
    mine = jnp.concatenate([own_ref[...], row_ref[...]], axis=1)
    return jnp.concatenate([mine, col_ref[...]], axis=0).astype(F32)


def qkv_part(hidden, gain, bias, w_own, w_oth, qvb_ref, x_ref, a_own, a_oth, q_ref, kv_ref):
    x_ref[...] = hidden
    normal, _ = statistics(hidden)
    normed = (normal * gain + bias).astype(BF)
    half = normed.shape[1] // 2
    left, right = normed[:, :half], normed[:, half:]
    a_own[...] = left
    a_oth[...] = right
    width = q_ref.shape[1]
    q_ref[...] = (mm(left, w_own[0]) + mm(right, w_oth[0]) + qvb_ref[0:1, :]).astype(BF)
    kv_ref[:, :width] = (mm(left, w_own[1]) + mm(right, w_oth[1])).astype(BF)
    kv_ref[:, width:] = (mm(left, w_own[2]) + mm(right, w_oth[2]) + qvb_ref[1:2, :]).astype(BF)


def param(par, name, layer):
    at = PARAMS.index(name) * LAYERS + layer
    return par[at : at + 1, :]


def first_kernel(layer, own, row, col, par, qvb, w_own, w_oth, *outs):
    hidden = pieces(own, row, col)
    qkv_part(
        hidden, param(par, "gain1", layer), param(par, "bias1", layer), w_own, w_oth, qvb, *outs
    )


def next_kernel(layer, x1, y_own, y_rec, par, qvb, w_own, w_oth, *outs):
    hidden = x1[...] + (both(y_own, y_rec) + param(par, "b_down", layer - 1))
    qkv_part(
        hidden, param(par, "gain1", layer), param(par, "bias1", layer), w_own, w_oth, qvb, *outs
    )


def attention_mask(info, seq_len, seq_own, seq_off, rows, cols):
    quarter = rows // 2
    i = lax.broadcasted_iota(jnp.int32, (rows, 1), 0)
    j = lax.broadcasted_iota(jnp.int32, (1, cols), 1)
    pos_q = jnp.where(i < quarter, info[1] + i, info[2] + i - quarter)
    pos_k = jnp.where(
        j < 2 * quarter,
        jnp.where(j < quarter, info[1] + j, info[2] + j - quarter),
        jnp.where(j < 3 * quarter, info[3] + j - 2 * quarter, info[4] + j - 3 * quarter),
    )
    offset = seq_off[...]
    inside = (
        (seq_own[...] == info[0]) & (pos_q >= offset) & (pos_q < offset + seq_len[...])
    )
    start = jnp.max(jnp.where(inside, offset, -1), axis=1, keepdims=True)
    start = jnp.where(start < 0, pos_q, start)
    return (pos_k <= pos_q) & (pos_k >= start)


def head_lanes(rows, which):
    lane = lax.broadcasted_iota(jnp.int32, (rows, 2 * DH), 1)
    return (lane < DH) if which == 0 else (lane >= DH)


def attend_kernel(
    info, seq_len, seq_own, seq_off, q, kv_own, kv_oth, o_ref, lse_ref
):
    rows, width = q.shape
    mask = attention_mask(info, seq_len, seq_own, seq_off, rows, 2 * rows)
    sides = [head_lanes(rows, 0), head_lanes(rows, 1)]
    lane = lax.broadcasted_iota(jnp.int32, (rows, 128), 1)
    logs = jnp.zeros((rows, 128), F32)
    scale = DH**-0.5
    for pair in range(width // (2 * DH)):
        span = slice(pair * 2 * DH, (pair + 1) * 2 * DH)
        vspan = slice(width + pair * 2 * DH, width + (pair + 1) * 2 * DH)
        queries = q[:, span] * jnp.asarray(scale, BF)
        keys = jnp.concatenate([kv_own[:, span], kv_oth[:, span]], axis=0)
        values = jnp.concatenate([kv_own[:, vspan], kv_oth[:, vspan]], axis=0)
        mixed = None
        for side in range(2):
            scores = mm_nt(jnp.where(sides[side], queries, jnp.zeros_like(queries)), keys)
            scores = jnp.where(mask, scores, MASKED_SCORE)
            largest = jnp.max(scores, axis=1, keepdims=True)
            powers = jnp.exp(scores - largest)
            total = jnp.sum(powers, axis=1, keepdims=True)
            out = mm((powers * (1.0 / total)).astype(BF), values)
            logs = jnp.where(lane == 2 * pair + side, largest + jnp.log(total), logs)
            mixed = out if side == 0 else jnp.where(sides[0], mixed, out)
        o_ref[:, span] = mixed.astype(BF)
    lse_ref[...] = logs


def mlp_kernel(
    layer, x, o_own, o_rec, par, wo_own, wo_oth, wc_own, wc_oth,
    bup, wu_own, wu_oth, wd_own, wd_oth,
    x1_ref, m_own, m_oth, h_ref, gp_ref, y_ref,
):
    mixed = o_own[...]
    quarter = o_rec.shape[0] // 2
    mixed_other = jnp.concatenate([o_rec[quarter:, :], o_rec[:quarter, :]], axis=0)
    attended = jnp.concatenate(
        [
            mm(mixed, wo_own[...]) + mm(mixed_other, wc_own[...]),
            mm(mixed, wo_oth[...]) + mm(mixed_other, wc_oth[...]),
        ],
        axis=1,
    )
    middle = x[...] + (attended + param(par, "b_out", layer))
    x1_ref[...] = middle
    normal, _ = statistics(middle)
    normed = (normal * param(par, "gain2", layer) + param(par, "bias2", layer)).astype(BF)
    half = normed.shape[1] // 2
    left, right = normed[:, :half], normed[:, half:]
    m_own[...] = left
    m_oth[...] = right
    width = h_ref.shape[1]
    step = 384
    out_own = out_oth = None
    for at in range(0, width, step):
        span = slice(at, at + step)
        upward = mm(left, wu_own[:, span]) + mm(right, wu_oth[:, span]) + bup[:, span]
        phi = 0.5 + 0.5 * lax.erf(upward * INV_SQRT2)
        density = jnp.exp(-0.5 * upward * upward) * INV_SQRT2PI
        active = (upward * phi).astype(BF)
        h_ref[:, span] = active
        gp_ref[:, span] = (phi + upward * density).astype(BF)
        part_own = mm(active, wd_own[span, :])
        part_oth = mm(active, wd_oth[span, :])
        out_own = part_own if out_own is None else out_own + part_own
        out_oth = part_oth if out_oth is None else out_oth + part_oth
    y_ref[:, :half] = out_own.astype(BF)
    y_ref[:, half:] = out_oth.astype(BF)


def mlp_back(
    grad, gp, wu_own, wu_oth, wd_own, wd_oth,
    g_ref, gy_own, gy_oth, du_ref, dm_ref, sdown_ref, sup_ref,
):
    g_ref[...] = grad
    branch = grad.astype(BF)
    half = branch.shape[1] // 2
    left, right = branch[:, :half], branch[:, half:]
    gy_own[...] = left
    gy_oth[...] = right
    sdown_ref[...] = col_sum(branch)
    width = gp.shape[1]
    step = 384
    out_own = out_oth = None
    for at in range(0, width, step):
        span = slice(at, at + step)
        grad_active = mm_nt(left, wd_own[span, :]) + mm_nt(right, wd_oth[span, :])
        grad_up = (grad_active * gp[:, span].astype(F32)).astype(BF)
        du_ref[:, span] = grad_up
        sup_ref[at // step : at // step + 1, :] = col_sum(grad_up)
        part_own = mm_nt(grad_up, wu_own[:, span])
        part_oth = mm_nt(grad_up, wu_oth[:, span])
        out_own = part_own if out_own is None else out_own + part_own
        out_oth = part_oth if out_oth is None else out_oth + part_oth
    dm_ref[:, :half] = out_own.astype(BF)
    dm_ref[:, half:] = out_oth.astype(BF)


def last_back_kernel(own, row, col, gp, wu_own, wu_oth, wd_own, wd_oth, *outs):
    mlp_back(pieces(own, row, col), gp, wu_own, wu_oth, wd_own, wd_oth, *outs)


def input_grad(layer, g1, da_own, da_rec, x, par, small_ref):
    grad_normed = both(da_own, da_rec)
    normal, inverse = statistics(x[...])
    small_ref[0:1, :] = col_sum(grad_normed * normal)
    small_ref[1:2, :] = col_sum(grad_normed)
    return g1[...] + norm_grad(
        grad_normed, normal, inverse, param(par, "gain1", layer)
    )


def next_back_kernel(
    layer, g1, da_own, da_rec, x, par, gp, wu_own, wu_oth, wd_own, wd_oth, small_ref, *outs
):
    grad = input_grad(layer + 1, g1, da_own, da_rec, x, par, small_ref)
    mlp_back(grad, gp, wu_own, wu_oth, wd_own, wd_oth, *outs)


def end_back_kernel(layer, g1, da_own, da_rec, x, par, own_ref, oth_ref):
    rows, width = da_own.shape
    grad_normed = da_own[...].astype(F32) + da_rec[...].astype(F32)
    normal, inverse = statistics(x[:rows, :])
    grad = g1[:rows, :] + norm_grad(grad_normed, normal, inverse, param(par, "gain1", layer))
    own_ref[...] = grad[:, : width // 2]
    oth_ref[...] = grad[:, width // 2 :]


def attend_back_kernel(
    layer, info, seq_len, seq_own, seq_off, grad, dm_own, dm_rec, x1, par, w_own, w_oth,
    q, kv_own, kv_oth, lse,
    g1_ref, ga_own, ga_oth, dq_ref, dkv_own, dkv_oth, small_ref,
):
    grad_normed = both(dm_own, dm_rec)
    normal, inverse = statistics(x1[...])
    grad_middle = grad[...] + norm_grad(
        grad_normed, normal, inverse, param(par, "gain2", layer)
    )
    g1_ref[...] = grad_middle
    branch = grad_middle.astype(BF)
    small_ref[0:1, :] = col_sum(branch)
    small_ref[1:2, :] = col_sum(grad_normed * normal)
    small_ref[2:3, :] = col_sum(grad_normed)
    half = branch.shape[1] // 2
    left, right = branch[:, :half], branch[:, half:]
    ga_own[...] = left
    ga_oth[...] = right
    grad_mixed = (mm_nt(left, w_own[...]) + mm_nt(right, w_oth[...])).astype(BF)
    rows, width = q.shape
    mask = attention_mask(info, seq_len, seq_own, seq_off, rows, 2 * rows)
    sides = [head_lanes(rows, 0), head_lanes(rows, 1)]
    key_sides = head_lanes(2 * rows, 0)
    scale = DH**-0.5
    for pair in range(width // (2 * DH)):
        span = slice(pair * 2 * DH, (pair + 1) * 2 * DH)
        vspan = slice(width + pair * 2 * DH, width + (pair + 1) * 2 * DH)
        queries = q[:, span] * jnp.asarray(scale, BF)
        keys = jnp.concatenate([kv_own[:, span], kv_oth[:, span]], axis=0)
        values = jnp.concatenate([kv_own[:, vspan], kv_oth[:, vspan]], axis=0)
        grad_out = grad_mixed[:, span]
        grad_q = grad_k = grad_v = None
        for side in range(2):
            head = 2 * pair + side
            scores = mm_nt(jnp.where(sides[side], queries, jnp.zeros_like(queries)), keys)
            scores = jnp.where(mask, scores, MASKED_SCORE)
            probability = jnp.exp(scores - lse[:, head : head + 1])
            grad_prob = mm_nt(jnp.where(sides[side], grad_out, jnp.zeros_like(grad_out)), values)
            inner = jnp.sum(grad_prob * probability, axis=1, keepdims=True)
            grad_scores = (probability * (grad_prob - inner)).astype(BF)
            part_q = mm(grad_scores, keys)
            part_k = mm_tn(grad_scores, queries)
            part_v = mm_tn(probability.astype(BF), grad_out)
            if side == 0:
                grad_q, grad_k, grad_v = part_q, part_k, part_v
            else:
                grad_q = jnp.where(sides[0], grad_q, part_q)
                grad_k = jnp.where(key_sides, grad_k, part_k)
                grad_v = jnp.where(key_sides, grad_v, part_v)
        dq_ref[:, span] = (grad_q * scale).astype(BF)
        dkv_own[:, span] = grad_k[:rows].astype(dkv_own.dtype)
        dkv_oth[:, span] = grad_k[rows:].astype(dkv_oth.dtype)
        dkv_own[:, vspan] = grad_v[:rows].astype(dkv_own.dtype)
        dkv_oth[:, vspan] = grad_v[rows:].astype(dkv_oth.dtype)


def project_back(dq, dkv_own, dkv_rec, w_own, w_oth, dkv_ref, small_ref):
    width = dq.shape[1]
    total = (dkv_own[...].astype(F32) + dkv_rec[...].astype(F32)).astype(BF)
    dkv_ref[...] = total
    small_ref[0:1, :] = col_sum(dq[...])
    small_ref[1:2, :] = col_sum(total[:, width:])
    parts = (dq[...], total[:, :width], total[:, width:])
    return [
        mm_nt(parts[0], weight[0]) + mm_nt(parts[1], weight[1]) + mm_nt(parts[2], weight[2])
        for weight in (w_own, w_oth)
    ]


def project_back_kernel(dq, dkv_own, dkv_rec, w_own, w_oth, dkv_ref, small_ref, da_ref):
    own, other = project_back(dq, dkv_own, dkv_rec, w_own, w_oth, dkv_ref, small_ref)
    half = own.shape[1]
    da_ref[:, :half] = own.astype(BF)
    da_ref[:, half:] = other.astype(BF)


def project_end_kernel(
    dq, dkv_own, dkv_rec, w_own, w_oth, x, dkv_ref, small_ref, keep_ref, send_ref, norm_ref
):
    own, other = project_back(dq, dkv_own, dkv_rec, w_own, w_oth, dkv_ref, small_ref)
    half = own.shape[1]
    rows = keep_ref.shape[0]
    normal, _ = statistics(x[...])
    for span, value in ((slice(0, half), own), (slice(half, 2 * half), other)):
        keep_ref[:, span] = value[:rows].astype(BF)
        send_ref[:, span] = value[rows:].astype(BF)
        norm_ref[0:1, span] = col_sum(value * normal[:, span])
        norm_ref[1:2, span] = col_sum(value)


def grad_term(left_own, left_rec, right_own, right_rec):
    return (mm_tn(left_own, right_own) + mm_tn(left_rec, right_rec)).astype(BF)


def put(side, half, at, value, keep_ref, send_ref):
    span = slice(at, at + value.shape[0])

    @pl.when(side == half)
    def _():
        keep_ref[span, :] = value

    @pl.when(side != half)
    def _():
        send_ref[span, :] = value


def mlp_grads(sides, h_own, h_rec, gy_own, gy_rec, m_own, m_rec, du_own, du_rec, keep, send):
    size = gy_own.shape[1]
    for k in range(h_own.shape[1] // size):
        span = slice(k * size, (k + 1) * size)
        down = grad_term(h_own[:, span], h_rec[:, span], gy_own[...], gy_rec[...])
        put(sides[0], 0, k * size, down, keep, send)
        up = grad_term(m_own[...], m_rec[...], du_own[:, span], du_rec[:, span])
        put(sides[0], 1, k * size, up, keep, send)


def attention_grads(
    sides, o_own, o_rec, ga_own, ga_rec, a_own, a_rec, dq_own, dq_rec, dkv_own, dkv_rec, *refs
):
    keep, send = refs[-3:-1]
    small = refs[-1]
    size = ga_own.shape[1]
    query = grad_term(a_own[...], a_rec[...], dq_own[...], dq_rec[...])
    put(sides[0], 0, 0, query, keep, send)
    for k in range(2):
        span = slice(k * size, (k + 1) * size)
        value = grad_term(a_own[...], a_rec[...], dkv_own[:, span], dkv_rec[:, span])
        put(sides[0], k, (1 - k) * size, value, keep, send)
    out = grad_term(o_own[...], o_rec[...], ga_own[...], ga_rec[...])
    put(sides[0], 1, size, out, keep, send)
    if len(refs) > 3:
        small[...] = jnp.zeros_like(small)
        at = 0
        for ref in refs[:-3]:
            count, width = ref.shape
            for part in range(width // size):
                small[at : at + count, :] = ref[:, part * size : (part + 1) * size]
                at += count
        half = small.shape[0] // 2
        for k in range(2):
            put(sides[0], k, 2 * size, small[k * half : (k + 1) * half, :].astype(BF), keep, send)


def added(keep, received):
    return (keep[...].astype(F32) + received[...].astype(F32)).astype(BF)


def halve_kernel(at, sides, *refs):
    keep, send = refs[-2:]
    parts = refs[:-2]
    sums = [added(parts[k], parts[k + 1]) for k in range(0, len(parts), 2)]
    total = sums[0] if len(sums) == 1 else jnp.concatenate(sums, axis=0)
    half = total.shape[0] // 2
    put(sides[at], 0, 0, total[:half], keep, send)
    put(sides[at], 1, 0, total[half:], keep, send)


def sum_kernel(mine, received, out_ref):
    out_ref[...] = added(mine, received)


def join_kernel(at, sides, mine, received, out_ref):
    half = mine.shape[0]

    @pl.when(sides[at] == 0)
    def _():
        out_ref[:half, :] = mine[...]
        out_ref[half:, :] = received[...]

    @pl.when(sides[at] != 0)
    def _():
        out_ref[:half, :] = received[...]
        out_ref[half:, :] = mine[...]


def write_mlp(low, high, up_ref, down_ref):
    down_ref[...] = low.astype(F32)
    size = down_ref.shape[1]
    for k in range(up_ref.shape[1] // size):
        span = slice(k * size, (k + 1) * size)
        up_ref[:, span] = high[span, :].astype(F32)


def write_attention(low, high, qkv_ref, out_ref):
    size = out_ref.shape[1]
    qkv_ref[0] = low[:size].astype(F32)
    qkv_ref[1] = low[size : 2 * size].astype(F32)
    qkv_ref[2] = high[:size].astype(F32)
    out_ref[...] = high[size : 2 * size].astype(F32)


def low_high(sides, mine, received):
    first = sides[0] == 0
    return jnp.where(first, mine[...], received[...]), jnp.where(first, received[...], mine[...])


def layer_result(sides, mine, received, up_ref, down_ref, qkv_ref, out_ref):
    low, high = low_high(sides, mine, received)
    cut = down_ref.shape[0]
    write_mlp(low[:cut], high[:cut], up_ref, down_ref)
    write_attention(low[cut:], high[cut:], qkv_ref, out_ref)


def mlp_result(sides, mine, received, *refs):
    write_mlp(*low_high(sides, mine, received), *refs[-2:])


def attention_result(sides, mine, received, *refs):
    qkv_ref, out_ref, small_ref = refs[-3:]
    low, high = low_high(sides, mine, received)
    write_attention(low, high, qkv_ref, out_ref)
    at = 2 * out_ref.shape[1]
    half = small_ref.shape[0] // 2
    small_ref[:half, :] = low[at:].astype(F32)
    small_ref[half:, :] = high[at:].astype(F32)


def small_kernel(mine, by_row, by_col, by_both, *outs):
    gain1, bias1, b_out, gain2, bias2, b_down, qvb, bup = outs
    count = mine.shape[0] // 2

    def split(layer, at, rows, out_at):
        own = slice(layer * count + at, layer * count + at + rows)
        other = slice(layer * count + at + rows, layer * count + at + 2 * rows)
        value = mine[own, :] + by_row[other, :]
        if layer == 0 and out_at == 0:
            value = value + (by_col[own, :] + by_both[other, :])
        return value

    for layer in range(LAYERS):
        norm = split(layer, 0, 2, 0)
        gain1[layer : layer + 1, :] = norm[0:1]
        bias1[layer : layer + 1, :] = norm[1:2]
        rest = split(layer, 4, 3, 1)
        b_out[layer : layer + 1, :] = rest[0:1]
        gain2[layer : layer + 1, :] = rest[1:2]
        bias2[layer : layer + 1, :] = rest[2:3]
        b_down[layer : layer + 1, :] = split(layer, 10, 1, 2)
        at = layer * count + 12
        qvb[layer] = mine[at : at + 2, :] + by_row[at : at + 2, :]
        last = mine[at + 2 : at + 6, :] + by_row[at + 2 : at + 6, :]
        size = last.shape[1]
        for k in range(4):
            bup[layer : layer + 1, k * size : (k + 1) * size] = last[k : k + 1]


SWAP = [(0, 1), (1, 0)]


def row_swap(operand):
    return lax.ppermute(operand, "row", SWAP)


def col_swap(operand):
    return lax.ppermute(operand, "col", SWAP)


def flipped(index, pairing):
    z, x, y = index // 8, (index // 2) % 4, index % 2
    if pairing == "za":
        z ^= 1
    elif pairing == "zb":
        z = 3 - z
    elif pairing == "xa":
        x ^= 1
    elif pairing == "xb":
        x = 3 - x
    else:
        y ^= 1
    return z * 8 + x * 2 + y


def side_of(index, pairing):
    z, x, y = index // 8, (index // 2) % 4, index % 2
    return {
        "za": (z + 1) // 2 % 2,
        "zb": z // 2,
        "xa": (x + 1) // 2 % 2,
        "xb": x // 2,
        "y": y,
    }[pairing]


def exchange(operand, pairings):
    table = [
        (dp * 2 + row, flipped(dp, pairings[row]) * 2 + row) for dp in range(32) for row in range(2)
    ]
    return lax.ppermute(operand, ("dp", "row"), table)


def my_side(pairings):
    dp = lax.axis_index("dp")
    return jnp.where(
        lax.axis_index("row") == 0, side_of(dp, pairings[0]), side_of(dp, pairings[1])
    )


Z_FIRST = [("za", "xa"), ("xa", "za"), ("zb", "xb"), ("xb", "zb"), ("y", "y")]
B_FIRST = [("zb", "xb"), ("xb", "zb"), ("za", "xa"), ("xa", "za"), ("y", "y")]


SMEM = pl.BlockSpec(memory_space=pltpu.SMEM)


class DataTotal:
    def __init__(self, order, sides, halvings):
        self.order, self.sides, self.halvings = order, sides, halvings
        self.parts, self.at = [], 0

    def start(self, keep, send):
        self.parts += [keep, exchange(send, self.order[0])]
        self.at = 1

    def step(self, after=()):
        at, count = self.at, len(self.order)
        rows = sum(part.shape[0] for part in self.parts[::2])
        width = self.parts[0].shape[1]
        if at < self.halvings:
            half = kept_of((rows // 2, width), BF)
            keep, send = call(
                partial(halve_kernel, at),
                [self.sides, *self.parts],
                [half, half],
                0,
                {0: SMEM},
                after,
            )
            pairings = self.order[at]
        elif at <= count:
            keep = send = call(sum_kernel, self.parts, [kept_of((rows, width), BF)], after=after)[0]
            pairings = self.order[at] if at < count else self.order[self.halvings - 1]
        else:
            back = self.halvings - 1 - (at - count - 1)
            keep = send = call(
                partial(join_kernel, back),
                [self.sides, *self.parts],
                [kept_of((2 * rows, width), BF)],
                0,
                {0: SMEM},
                after,
            )[0]
            pairings = self.order[back - 1]
        self.parts = [keep, exchange(send, pairings)]
        self.at += 1
        return send

    @property
    def left(self):
        return len(self.order) + self.halvings - self.at


def body(
    tokens,
    cotangent,
    ln1_gain,
    ln1_bias,
    w_qkv,
    qv_bias,
    w_out,
    b_out,
    ln2_gain,
    ln2_bias,
    w_up,
    b_up,
    w_down,
    b_down,
    seq_lengths,
    seq_owner,
    seq_offset,
):
    row = lax.axis_index("row")
    col = lax.axis_index("col")
    block, half = tokens.shape
    part = block // 2
    rows = block
    width = 2 * half
    hidden_part = w_up.shape[2]

    def split_input(operand):
        own = lax.dynamic_slice_in_dim(operand, row * part, part, 0)
        sent = lax.dynamic_slice_in_dim(operand, (1 - row) * part, part, 0)
        received = row_swap(sent)
        across = col_swap(jnp.concatenate([own, received], axis=1))
        return own, received, across

    token_parts = split_input(tokens)
    params = jnp.concatenate([ln1_gain, ln1_bias, b_out, ln2_gain, ln2_bias, b_down], axis=0)
    params = jnp.concatenate([params, row_swap(params)], axis=1)
    wq = jnp.transpose(w_qkv, (0, 2, 1, 3))
    wq_oth = row_swap(wq)
    wo_oth = row_swap(w_out)
    wu_oth = row_swap(w_up)
    wd_oth = row_swap(w_down)
    wc_own = col_swap(lax.optimization_barrier((w_out, token_parts[2]))[0])
    wc_oth = row_swap(wc_own)
    cot_parts = split_input(cotangent)
    bup = b_up[:, None, :]
    info = jnp.stack(
        [
            lax.axis_index("dp"),
            col * block + row * part,
            (1 - col) * block + row * part,
            col * block + (1 - row) * part,
            (1 - col) * block + (1 - row) * part,
        ]
    ).astype(jnp.int32)
    seqs = (info, seq_lengths[None, :], seq_owner[None, :], seq_offset[None, :])
    smem = SMEM
    head_width = w_qkv.shape[3]
    full_kept = kept_of((rows, width), BF)
    act_kept = kept_of((rows, half), BF)
    stream_kept = kept_of((rows, width), F32)
    wide_kept = kept_of((rows, hidden_part), BF)

    kept = []
    x1 = y_down = y_down_rec = None
    for l in range(LAYERS):
        outs = [stream_kept, act_kept, act_kept, act_kept, full_kept]
        if l == 0:
            ins = [*token_parts, params, qv_bias, wq, wq_oth]
            kernel = partial(first_kernel, l)
        else:
            ins = [x1, y_down, y_down_rec, params, qv_bias, wq, wq_oth]
            kernel = partial(next_kernel, l)
        spec = {k: layer_spec(ins[k], l) for k in (4, 5, 6)}
        x, a_own, a_oth, q, kv = call(kernel, ins, outs, 2 * rows * width * 3 * half, spec)
        kv_rec = row_swap(kv)
        a_rec = row_swap(a_oth)
        ins = [*seqs, q, kv, kv_rec]
        o, lse = call(
            attend_kernel,
            ins,
            [act_kept, kept_of((rows, 128), F32)],
            2 * rows * width * half * 2,
            {0: smem},
        )
        o_across = col_swap(o)
        o_rec = row_swap(o)
        ins = [x, o, o_across, params, w_out, wo_oth, wc_own, wc_oth]
        ins += [bup, w_up, wu_oth, w_down, wd_oth]
        spec = {k: layer_spec(ins[k], l) for k in range(4, 13)}
        x1, m_own, m_oth, h, gp, y_down = call(
            partial(mlp_kernel, l),
            ins,
            [stream_kept, act_kept, act_kept, wide_kept, wide_kept, full_kept],
            4 * rows * width * hidden_part,
            spec,
        )
        m_rec = row_swap(m_oth)
        h_rec = row_swap(h)
        if l < LAYERS - 1:
            y_down_rec = col_swap(y_down)
        kept.append((x, a_own, a_rec, q, kv, kv_rec, o, o_rec, lse, x1, m_own, m_rec, h, h_rec, gp))

    y_last = col_swap(y_down[part:])
    out_rows = x1[:part] + (
        y_down[:part].astype(F32) + y_last.astype(F32) + params[-1:, :]
    )
    out_other = row_swap(out_rows[:, half:])
    out_own = out_rows[:, :half]

    def by_row(own, other):
        return jnp.where(
            row == 0, jnp.concatenate([own, other]), jnp.concatenate([other, own])
        )

    out_act = by_row(out_own, out_other)

    flops = rows * width * half
    z_sides = jnp.stack([my_side(p) for p in Z_FIRST]).astype(jnp.int32)
    b_sides = jnp.stack([my_side(p) for p in B_FIRST]).astype(jnp.int32)

    def mlp_total(layer, sides, gy_own, gy_rec, du, du_rec, after=()):
        h, h_rec, m_own, m_rec = (kept[layer][k] for k in (12, 13, 10, 11))
        return call(
            mlp_grads,
            [sides, h, h_rec, gy_own, gy_rec, m_own, m_rec, du, du_rec],
            [kept_of((4 * half, half), BF)] * 2,
            4 * rows * half * half * 8,
            {0: smem},
            after,
        )

    def attention_total(layer, sides, ins, smalls=(), after=()):
        a_own, a_rec, o, o_rec = (kept[layer][k] for k in (1, 2, 6, 7))
        ga_own, ga_rec, dq, dq_rec, dkv, dkv_rec = ins
        extra = SMALL_ROWS // 2 if smalls else 0
        return call(
            attention_grads,
            [sides, o, o_rec, ga_own, ga_rec, a_own, a_rec, dq, dq_rec, dkv, dkv_rec, *smalls],
            [kept_of((2 * half + extra, half), BF)] * 2,
            4 * rows * half * half * 4,
            {0: smem},
            after,
            scratch=[pltpu.VMEM((SMALL_ROWS, half), F32)],
        )

    def mlp_stage(layer, kernel, ins, outs, after):
        first = len(ins)
        ins = ins + [kept[layer][14], w_up, wu_oth, w_down, wd_oth]
        spec = {k: layer_spec(ins[k], layer) for k in range(first + 1, first + 5)}
        return call(kernel, ins, outs, 4 * flops * 4, spec, after)

    def attend_stage(layer, g, dm, dm_rec, after):
        x1, q, kv, kv_rec, lse = (kept[layer][k] for k in (9, 3, 4, 5, 8))
        ins = [*seqs, g, dm, dm_rec, x1, params, w_out, wo_oth, q, kv, kv_rec, lse]
        spec = {0: smem, 9: layer_spec(w_out, layer), 10: layer_spec(wo_oth, layer)}
        return call(
            partial(attend_back_kernel, layer),
            ins,
            [
                stream_kept,
                act_kept,
                act_kept,
                act_kept,
                full_kept,
                full_kept,
                shape_of((3, width), F32),
            ],
            6 * flops,
            spec,
            after,
        )

    def project_stage(layer, kernel, ins, outs, after=()):
        ins = [*ins[:3], wq, wq_oth, *ins[3:]]
        spec = {3: layer_spec(wq, layer), 4: layer_spec(wq_oth, layer)}
        outs = [full_kept, shape_of((2, half), F32)] + outs
        return call(kernel, ins, outs, 6 * flops, spec, after)

    outs = [
        stream_kept,
        act_kept,
        act_kept,
        wide_kept,
        full_kept,
        shape_of((1, width), F32),
        shape_of((hidden_part // half, half), F32),
    ]
    layer_one = DataTotal(Z_FIRST, z_sides, 3)
    mlp_zero = DataTotal(B_FIRST, b_sides, 3)
    attention_zero = DataTotal(Z_FIRST, z_sides, 2)
    g, gy_own, gy_oth, du, dm, s_down1, s_up1 = mlp_stage(
        1, last_back_kernel, list(cot_parts), outs, ()
    )
    dm_rec, gy_rec, du_rec = col_swap(dm), row_swap(gy_oth), row_swap(du)
    keep, send = mlp_total(1, z_sides, gy_own, gy_rec, du, du_rec)
    layer_one.start(keep, send)
    g1, ga_own, ga_oth, dq, dkv, dkv_oth, s_att1 = attend_stage(1, g, dm, dm_rec, (send,))
    dkv_rec, ga_rec, dq_rec = row_swap(dkv_oth), row_swap(ga_oth), row_swap(dq)
    dkv_total, s_qv1, da = project_stage(1, project_back_kernel, [dq, dkv, dkv_rec], [full_kept])
    da_rec, dkv_total_rec = col_swap(da), row_swap(dkv_total)
    keep, send = attention_total(
        1, z_sides, [ga_own, ga_rec, dq, dq_rec, dkv_total, dkv_total_rec]
    )
    layer_one.start(keep, send)
    s_ln1, g, gy_own, gy_oth, du, dm, s_down0, s_up0 = mlp_stage(
        0,
        partial(next_back_kernel, 0),
        [g1, da, da_rec, kept[1][0], params],
        [shape_of((2, width), F32)] + outs,
        (send,),
    )
    dm_rec, gy_rec, du_rec = col_swap(dm), row_swap(gy_oth), row_swap(du)
    sent = layer_one.step((dm,))
    keep, send = mlp_total(0, b_sides, gy_own, gy_rec, du, du_rec, (sent,))
    mlp_zero.start(keep, send)
    g1, ga_own, ga_oth, dq, dkv, dkv_oth, s_att0 = attend_stage(0, g, dm, dm_rec, (send,))
    dkv_rec, ga_rec, dq_rec = row_swap(dkv_oth), row_swap(ga_oth), row_swap(dq)
    dkv_total, s_qv0, da_keep, da_send, s_ln0 = project_stage(
        0,
        project_end_kernel,
        [dq, dkv, dkv_rec, kept[0][0]],
        [kept_of((part, width), BF)] * 2 + [shape_of((2, width), F32)],
    )
    da_rec, dkv_total_rec = col_swap(da_send), row_swap(dkv_total)
    smalls = [s_ln0, s_att0, s_down0, s_qv0, s_up0, s_ln1, s_att1, s_down1, s_qv1, s_up1]
    keep, send = attention_total(
        0, z_sides, [ga_own, ga_rec, dq, dq_rec, dkv_total, dkv_total_rec], smalls
    )
    attention_zero.start(keep, send)
    sent = layer_one.step((send,))
    sent = mlp_zero.step((sent,))
    grad_own, grad_oth = call(
        partial(end_back_kernel, 0),
        [g1, da_keep, da_rec, kept[0][0], params],
        [kept_of((part, half), F32)] * 2,
        after=(sent,),
    )
    grad_tokens = by_row(grad_own, row_swap(grad_oth))
    sent = grad_own
    while attention_zero.left > 0 or mlp_zero.left > 0 or layer_one.left > 0:
        for total in (attention_zero, layer_one, mlp_zero):
            if total.left > 0:
                sent = total.step((sent,))

    def result(kernel, total, layer, shapes, before, extra=()):
        ins = [total.sides, *total.parts, *before]
        specs = {0: smem}
        for k in range(3, len(ins)):
            specs[k] = pl.BlockSpec(memory_space=pl.ANY)
        aliases = {3 + k: k for k in range(len(before))}
        outs = [(shape, layer_spec(shape, layer)) for shape in shapes] + list(extra)
        return call(kernel, ins, outs, 0, specs, aliases=aliases)

    up, down, qkv, out = result(
        layer_result,
        layer_one,
        1,
        [kept_of(x.shape, F32) for x in (w_up, w_down, wq, w_out)],
        [],
    )
    grad_up, grad_down = result(
        mlp_result, mlp_zero, 0, [kept_of(x.shape, F32) for x in (w_up, w_down)], [up, down]
    )
    grad_qkv, grad_out, small = result(
        attention_result,
        attention_zero,
        0,
        [kept_of(x.shape, F32) for x in (wq, w_out)],
        [qkv, out],
        [shape_of((SMALL_ROWS, half), F32)],
    )
    grad_qkv = jnp.transpose(grad_qkv, (0, 2, 1, 3))
    small = small[:36]
    across = lax.ppermute(small, ("row", "col"), [(k, 3 - k) for k in range(4)])
    vector = shape_of((LAYERS, half), F32)
    g_gain1, g_bias1, g_bout, g_gain2, g_bias2, g_bdown, g_qvb, g_bup = call(
        small_kernel,
        [small, row_swap(small), col_swap(small), across],
        [vector] * 6 + [shape_of(qv_bias.shape, F32), shape_of(b_up.shape, F32)],
    )
    return (
        out_act,
        grad_tokens,
        g_gain1,
        g_bias1,
        grad_qkv,
        g_qvb,
        grad_out,
        g_bout,
        g_gain2,
        g_bias2,
        grad_up,
        g_bup,
        grad_down,
        g_bdown,
    )


def solution(mesh):
    in_specs = (
        P(("dp", "col"), "row"),
        P(("dp", "col"), "row"),
        P(None, "row"),
        P(None, "row"),
        P(None, "row", None, "col"),
        P(None, None, "col"),
        P(None, "col", "row"),
        P(None, "row"),
        P(None, "row"),
        P(None, "row"),
        P(None, "row", "col"),
        P(None, "col"),
        P(None, "col", "row"),
        P(None, "row"),
        P(),
        P(),
        P(),
    )
    out_specs = (
        P(("dp", "col"), "row"),
        P(("dp", "col"), "row"),
        P(None, "row"),
        P(None, "row"),
        P(None, "row", None, "col"),
        P(None, None, "col"),
        P(None, "col", "row"),
        P(None, "row"),
        P(None, "row"),
        P(None, "row"),
        P(None, "row", "col"),
        P(None, "col"),
        P(None, "col", "row"),
        P(None, "row"),
    )
    return jax.shard_map(body, mesh=mesh, in_specs=in_specs, out_specs=out_specs, check_vma=False)
```

```python
import math
from functools import partial

import jax
import jax.numpy as jnp
from jax import lax
from jax.experimental import pallas as pl
from jax.experimental.pallas import tpu as pltpu
from jax.sharding import PartitionSpec as P

DH = 64
LAYERS = 2
EPSILON = 1e-05
MASKED_SCORE = -1e30
INV_SQRT2 = 0.7071067811865476
INV_SQRT2PI = 0.3989422804014327
BF = jnp.bfloat16
F32 = jnp.float32
VMEM_BYTES = 32 * 1024 * 1024
VMEM_EXTRA = 4 * 1024 * 1024


SMALL_ROWS = 64
PARAMS = ("gain1", "bias1", "b_out", "gain2", "bias2", "b_down")


def call(kernel, ins, outs, flops=0, specs=None, after=(), aliases=None, scratch=()):
    count = len(ins)

    def run(*refs):
        kernel(*refs[:count], *refs[count + len(after) :])

    in_specs = []
    placed = []
    for position, operand in enumerate(ins):
        spec = (specs or {}).get(position)
        in_specs.append(spec if spec is not None else whole_spec(operand))
        placed.append(operand)
    in_specs += [pl.BlockSpec(memory_space=pl.ANY)] * len(after)
    out_specs = [x[1] if isinstance(x, tuple) else whole_spec(x) for x in outs]
    outs = [x[0] if isinstance(x, tuple) else x for x in outs]
    size = sum(math.prod(x.shape) * x.dtype.itemsize for x in (*ins, *outs))
    return pl.pallas_call(
        run,
        out_shape=outs,
        in_specs=in_specs,
        out_specs=out_specs,
        grid=(1,),
        input_output_aliases=aliases or {},
        scratch_shapes=list(scratch),
        compiler_params=pltpu.CompilerParams(vmem_limit_bytes=min(VMEM_BYTES, size + size // 2 + VMEM_EXTRA)),
        cost_estimate=pl.CostEstimate(flops=flops, bytes_accessed=size, transcendentals=0),
    )(*placed, *after)


def whole_spec(operand):
    zeros = (0,) * len(operand.shape)
    return pl.BlockSpec(operand.shape, lambda i: zeros)


def layer_spec(operand, layer):
    rest = operand.shape[1:]
    zeros = (0,) * len(rest)
    return pl.BlockSpec((None,) + rest, lambda i: (layer,) + zeros)


def shape_of(shape, dtype):
    return jax.ShapeDtypeStruct(shape, dtype)


def kept_of(shape, dtype):
    return jax.ShapeDtypeStruct(shape, dtype)


def mm(left, right):
    return jnp.dot(left, right, preferred_element_type=F32)


def mm_nt(left, right):
    return lax.dot_general(left, right, (((1,), (1,)), ((), ())), preferred_element_type=F32)


def mm_tn(left, right):
    return lax.dot_general(left, right, (((0,), (0,)), ((), ())), preferred_element_type=F32)


def swapped(ref):
    half = ref.shape[0] // 2
    return jnp.concatenate([ref[half:, :], ref[:half, :]], axis=0).astype(F32)


def both(own_ref, received_ref):
    return own_ref[...].astype(F32) + swapped(received_ref)


def statistics(inputs):
    center = jnp.mean(inputs, axis=1, keepdims=True)
    second = jnp.mean(inputs * inputs, axis=1, keepdims=True)
    inverse = lax.rsqrt(second - center * center + EPSILON)
    return (inputs - center) * inverse, inverse


def norm_grad(grad_norm, normal, inverse, gain):
    scaled = grad_norm * gain
    first = jnp.mean(scaled, axis=1, keepdims=True)
    second = jnp.mean(scaled * normal, axis=1, keepdims=True)
    return inverse * (scaled - first - normal * second)


def col_sum(values):
    return jnp.sum(values.astype(F32), axis=0, keepdims=True)


def pieces(own_ref, row_ref, col_ref):
    mine = jnp.concatenate([own_ref[...], row_ref[...]], axis=1)
    return jnp.concatenate([mine, col_ref[...]], axis=0).astype(F32)


def qkv_part(hidden, gain, bias, w_own, w_oth, qvb_ref, x_ref, a_own, a_oth, q_ref, kv_ref):
    x_ref[...] = hidden
    normal, _ = statistics(hidden)
    normed = (normal * gain + bias).astype(BF)
    half = normed.shape[1] // 2
    left, right = normed[:, :half], normed[:, half:]
    a_own[...] = left
    a_oth[...] = right
    width = q_ref.shape[1]
    q_ref[...] = (mm(left, w_own[0]) + mm(right, w_oth[0]) + qvb_ref[0:1, :]).astype(BF)
    kv_ref[:, :width] = (mm(left, w_own[1]) + mm(right, w_oth[1])).astype(BF)
    kv_ref[:, width:] = (mm(left, w_own[2]) + mm(right, w_oth[2]) + qvb_ref[1:2, :]).astype(BF)


def param(par, name, layer):
    at = PARAMS.index(name) * LAYERS + layer
    return par[at : at + 1, :]


def first_kernel(layer, own, row, col, par, qvb, w_own, w_oth, *outs):
    hidden = pieces(own, row, col)
    qkv_part(
        hidden, param(par, "gain1", layer), param(par, "bias1", layer), w_own, w_oth, qvb, *outs
    )


def next_kernel(layer, x1, y_own, y_rec, par, qvb, w_own, w_oth, *outs):
    hidden = x1[...] + (both(y_own, y_rec) + param(par, "b_down", layer - 1))
    qkv_part(
        hidden, param(par, "gain1", layer), param(par, "bias1", layer), w_own, w_oth, qvb, *outs
    )


def attention_mask(info, seq_len, seq_own, seq_off, rows, cols):
    quarter = rows // 2
    i = lax.broadcasted_iota(jnp.int32, (rows, 1), 0)
    j = lax.broadcasted_iota(jnp.int32, (1, cols), 1)
    pos_q = jnp.where(i < quarter, info[1] + i, info[2] + i - quarter)
    pos_k = jnp.where(
        j < 2 * quarter,
        jnp.where(j < quarter, info[1] + j, info[2] + j - quarter),
        jnp.where(j < 3 * quarter, info[3] + j - 2 * quarter, info[4] + j - 3 * quarter),
    )
    offset = seq_off[...]
    inside = (
        (seq_own[...] == info[0]) & (pos_q >= offset) & (pos_q < offset + seq_len[...])
    )
    start = jnp.max(jnp.where(inside, offset, -1), axis=1, keepdims=True)
    start = jnp.where(start < 0, pos_q, start)
    return (pos_k <= pos_q) & (pos_k >= start)


def head_lanes(rows, which):
    lane = lax.broadcasted_iota(jnp.int32, (rows, 2 * DH), 1)
    return (lane < DH) if which == 0 else (lane >= DH)


def attend_kernel(
    info, seq_len, seq_own, seq_off, q, kv_own, kv_oth, o_ref, lse_ref
):
    rows, width = q.shape
    mask = attention_mask(info, seq_len, seq_own, seq_off, rows, 2 * rows)
    sides = [head_lanes(rows, 0), head_lanes(rows, 1)]
    lane = lax.broadcasted_iota(jnp.int32, (rows, 128), 1)
    logs = jnp.zeros((rows, 128), F32)
    scale = DH**-0.5
    for pair in range(width // (2 * DH)):
        span = slice(pair * 2 * DH, (pair + 1) * 2 * DH)
        vspan = slice(width + pair * 2 * DH, width + (pair + 1) * 2 * DH)
        queries = q[:, span] * jnp.asarray(scale, BF)
        keys = jnp.concatenate([kv_own[:, span], kv_oth[:, span]], axis=0)
        values = jnp.concatenate([kv_own[:, vspan], kv_oth[:, vspan]], axis=0)
        mixed = None
        for side in range(2):
            scores = mm_nt(jnp.where(sides[side], queries, jnp.zeros_like(queries)), keys)
            scores = jnp.where(mask, scores, MASKED_SCORE)
            largest = jnp.max(scores, axis=1, keepdims=True)
            powers = jnp.exp(scores - largest)
            total = jnp.sum(powers, axis=1, keepdims=True)
            out = mm((powers * (1.0 / total)).astype(BF), values)
            logs = jnp.where(lane == 2 * pair + side, largest + jnp.log(total), logs)
            mixed = out if side == 0 else jnp.where(sides[0], mixed, out)
        o_ref[:, span] = mixed.astype(BF)
    lse_ref[...] = logs


def mlp_kernel(
    layer, x, o_own, o_rec, par, wo_own, wo_oth, wc_own, wc_oth,
    bup, wu_own, wu_oth, wd_own, wd_oth,
    x1_ref, m_own, m_oth, h_ref, gp_ref, y_ref,
):
    mixed = o_own[...]
    quarter = o_rec.shape[0] // 2
    mixed_other = jnp.concatenate([o_rec[quarter:, :], o_rec[:quarter, :]], axis=0)
    attended = jnp.concatenate(
        [
            mm(mixed, wo_own[...]) + mm(mixed_other, wc_own[...]),
            mm(mixed, wo_oth[...]) + mm(mixed_other, wc_oth[...]),
        ],
        axis=1,
    )
    middle = x[...] + (attended + param(par, "b_out", layer))
    x1_ref[...] = middle
    normal, _ = statistics(middle)
    normed = (normal * param(par, "gain2", layer) + param(par, "bias2", layer)).astype(BF)
    half = normed.shape[1] // 2
    left, right = normed[:, :half], normed[:, half:]
    m_own[...] = left
    m_oth[...] = right
    width = h_ref.shape[1]
    step = 384
    out_own = out_oth = None
    for at in range(0, width, step):
        span = slice(at, at + step)
        upward = mm(left, wu_own[:, span]) + mm(right, wu_oth[:, span]) + bup[:, span]
        phi = 0.5 + 0.5 * lax.erf(upward * INV_SQRT2)
        density = jnp.exp(-0.5 * upward * upward) * INV_SQRT2PI
        active = (upward * phi).astype(BF)
        h_ref[:, span] = active
        gp_ref[:, span] = (phi + upward * density).astype(BF)
        part_own = mm(active, wd_own[span, :])
        part_oth = mm(active, wd_oth[span, :])
        out_own = part_own if out_own is None else out_own + part_own
        out_oth = part_oth if out_oth is None else out_oth + part_oth
    y_ref[:, :half] = out_own.astype(BF)
    y_ref[:, half:] = out_oth.astype(BF)


def mlp_back(
    grad, gp, wu_own, wu_oth, wd_own, wd_oth,
    g_ref, gy_own, gy_oth, du_ref, dm_ref, sdown_ref, sup_ref,
):
    g_ref[...] = grad
    branch = grad.astype(BF)
    half = branch.shape[1] // 2
    left, right = branch[:, :half], branch[:, half:]
    gy_own[...] = left
    gy_oth[...] = right
    sdown_ref[...] = col_sum(branch)
    width = gp.shape[1]
    step = 384
    out_own = out_oth = None
    for at in range(0, width, step):
        span = slice(at, at + step)
        grad_active = mm_nt(left, wd_own[span, :]) + mm_nt(right, wd_oth[span, :])
        grad_up = (grad_active * gp[:, span].astype(F32)).astype(BF)
        du_ref[:, span] = grad_up
        sup_ref[at // step : at // step + 1, :] = col_sum(grad_up)
        part_own = mm_nt(grad_up, wu_own[:, span])
        part_oth = mm_nt(grad_up, wu_oth[:, span])
        out_own = part_own if out_own is None else out_own + part_own
        out_oth = part_oth if out_oth is None else out_oth + part_oth
    dm_ref[:, :half] = out_own.astype(BF)
    dm_ref[:, half:] = out_oth.astype(BF)


def last_back_kernel(own, row, col, gp, wu_own, wu_oth, wd_own, wd_oth, *outs):
    mlp_back(pieces(own, row, col), gp, wu_own, wu_oth, wd_own, wd_oth, *outs)


def input_grad(layer, g1, da_own, da_rec, x, par, small_ref):
    grad_normed = both(da_own, da_rec)
    normal, inverse = statistics(x[...])
    small_ref[0:1, :] = col_sum(grad_normed * normal)
    small_ref[1:2, :] = col_sum(grad_normed)
    return g1[...] + norm_grad(
        grad_normed, normal, inverse, param(par, "gain1", layer)
    )


def next_back_kernel(
    layer, g1, da_own, da_rec, x, par, gp, wu_own, wu_oth, wd_own, wd_oth, small_ref, *outs
):
    grad = input_grad(layer + 1, g1, da_own, da_rec, x, par, small_ref)
    mlp_back(grad, gp, wu_own, wu_oth, wd_own, wd_oth, *outs)


def end_back_kernel(layer, g1, da_own, da_rec, x, par, own_ref, oth_ref):
    rows, width = da_own.shape
    grad_normed = da_own[...].astype(F32) + da_rec[...].astype(F32)
    normal, inverse = statistics(x[:rows, :])
    grad = g1[:rows, :] + norm_grad(grad_normed, normal, inverse, param(par, "gain1", layer))
    own_ref[...] = grad[:, : width // 2]
    oth_ref[...] = grad[:, width // 2 :]


def attend_back_kernel(
    layer, info, seq_len, seq_own, seq_off, grad, dm_own, dm_rec, x1, par, w_own, w_oth,
    q, kv_own, kv_oth, lse,
    g1_ref, ga_own, ga_oth, dq_ref, dkv_own, dkv_oth, small_ref,
):
    grad_normed = both(dm_own, dm_rec)
    normal, inverse = statistics(x1[...])
    grad_middle = grad[...] + norm_grad(
        grad_normed, normal, inverse, param(par, "gain2", layer)
    )
    g1_ref[...] = grad_middle
    branch = grad_middle.astype(BF)
    small_ref[0:1, :] = col_sum(branch)
    small_ref[1:2, :] = col_sum(grad_normed * normal)
    small_ref[2:3, :] = col_sum(grad_normed)
    half = branch.shape[1] // 2
    left, right = branch[:, :half], branch[:, half:]
    ga_own[...] = left
    ga_oth[...] = right
    grad_mixed = (mm_nt(left, w_own[...]) + mm_nt(right, w_oth[...])).astype(BF)
    rows, width = q.shape
    mask = attention_mask(info, seq_len, seq_own, seq_off, rows, 2 * rows)
    sides = [head_lanes(rows, 0), head_lanes(rows, 1)]
    key_sides = head_lanes(2 * rows, 0)
    scale = DH**-0.5
    for pair in range(width // (2 * DH)):
        span = slice(pair * 2 * DH, (pair + 1) * 2 * DH)
        vspan = slice(width + pair * 2 * DH, width + (pair + 1) * 2 * DH)
        queries = q[:, span] * jnp.asarray(scale, BF)
        keys = jnp.concatenate([kv_own[:, span], kv_oth[:, span]], axis=0)
        values = jnp.concatenate([kv_own[:, vspan], kv_oth[:, vspan]], axis=0)
        grad_out = grad_mixed[:, span]
        grad_q = grad_k = grad_v = None
        for side in range(2):
            head = 2 * pair + side
            scores = mm_nt(jnp.where(sides[side], queries, jnp.zeros_like(queries)), keys)
            scores = jnp.where(mask, scores, MASKED_SCORE)
            probability = jnp.exp(scores - lse[:, head : head + 1])
            grad_prob = mm_nt(jnp.where(sides[side], grad_out, jnp.zeros_like(grad_out)), values)
            inner = jnp.sum(grad_prob * probability, axis=1, keepdims=True)
            grad_scores = (probability * (grad_prob - inner)).astype(BF)
            part_q = mm(grad_scores, keys)
            part_k = mm_tn(grad_scores, queries)
            part_v = mm_tn(probability.astype(BF), grad_out)
            if side == 0:
                grad_q, grad_k, grad_v = part_q, part_k, part_v
            else:
                grad_q = jnp.where(sides[0], grad_q, part_q)
                grad_k = jnp.where(key_sides, grad_k, part_k)
                grad_v = jnp.where(key_sides, grad_v, part_v)
        dq_ref[:, span] = (grad_q * scale).astype(BF)
        dkv_own[:, span] = grad_k[:rows].astype(dkv_own.dtype)
        dkv_oth[:, span] = grad_k[rows:].astype(dkv_oth.dtype)
        dkv_own[:, vspan] = grad_v[:rows].astype(dkv_own.dtype)
        dkv_oth[:, vspan] = grad_v[rows:].astype(dkv_oth.dtype)


def project_back(dq, dkv_own, dkv_rec, w_own, w_oth, dkv_ref, small_ref):
    width = dq.shape[1]
    total = (dkv_own[...].astype(F32) + dkv_rec[...].astype(F32)).astype(BF)
    dkv_ref[...] = total
    small_ref[0:1, :] = col_sum(dq[...])
    small_ref[1:2, :] = col_sum(total[:, width:])
    parts = (dq[...], total[:, :width], total[:, width:])
    return [
        mm_nt(parts[0], weight[0]) + mm_nt(parts[1], weight[1]) + mm_nt(parts[2], weight[2])
        for weight in (w_own, w_oth)
    ]


def project_back_kernel(dq, dkv_own, dkv_rec, w_own, w_oth, dkv_ref, small_ref, da_ref):
    own, other = project_back(dq, dkv_own, dkv_rec, w_own, w_oth, dkv_ref, small_ref)
    half = own.shape[1]
    da_ref[:, :half] = own.astype(BF)
    da_ref[:, half:] = other.astype(BF)


def project_end_kernel(
    dq, dkv_own, dkv_rec, w_own, w_oth, x, dkv_ref, small_ref, keep_ref, send_ref, norm_ref
):
    own, other = project_back(dq, dkv_own, dkv_rec, w_own, w_oth, dkv_ref, small_ref)
    half = own.shape[1]
    rows = keep_ref.shape[0]
    normal, _ = statistics(x[...])
    for span, value in ((slice(0, half), own), (slice(half, 2 * half), other)):
        keep_ref[:, span] = value[:rows].astype(BF)
        send_ref[:, span] = value[rows:].astype(BF)
        norm_ref[0:1, span] = col_sum(value * normal[:, span])
        norm_ref[1:2, span] = col_sum(value)


def grad_term(left_own, left_rec, right_own, right_rec):
    return (mm_tn(left_own, right_own) + mm_tn(left_rec, right_rec)).astype(BF)


def put(side, half, at, value, keep_ref, send_ref):
    span = slice(at, at + value.shape[0])

    @pl.when(side == half)
    def _():
        keep_ref[span, :] = value

    @pl.when(side != half)
    def _():
        send_ref[span, :] = value


def mlp_grads(sides, h_own, h_rec, gy_own, gy_rec, m_own, m_rec, du_own, du_rec, keep, send):
    size = gy_own.shape[1]
    for k in range(h_own.shape[1] // size):
        span = slice(k * size, (k + 1) * size)
        down = grad_term(h_own[:, span], h_rec[:, span], gy_own[...], gy_rec[...])
        put(sides[0], 0, k * size, down, keep, send)
        up = grad_term(m_own[...], m_rec[...], du_own[:, span], du_rec[:, span])
        put(sides[0], 1, k * size, up, keep, send)


def attention_grads(
    sides, o_own, o_rec, ga_own, ga_rec, a_own, a_rec, dq_own, dq_rec, dkv_own, dkv_rec, *refs
):
    keep, send = refs[-3:-1]
    small = refs[-1]
    size = ga_own.shape[1]
    query = grad_term(a_own[...], a_rec[...], dq_own[...], dq_rec[...])
    put(sides[0], 0, 0, query, keep, send)
    for k in range(2):
        span = slice(k * size, (k + 1) * size)
        value = grad_term(a_own[...], a_rec[...], dkv_own[:, span], dkv_rec[:, span])
        put(sides[0], k, (1 - k) * size, value, keep, send)
    out = grad_term(o_own[...], o_rec[...], ga_own[...], ga_rec[...])
    put(sides[0], 1, size, out, keep, send)
    if len(refs) > 3:
        small[...] = jnp.zeros_like(small)
        at = 0
        for ref in refs[:-3]:
            count, width = ref.shape
            for part in range(width // size):
                small[at : at + count, :] = ref[:, part * size : (part + 1) * size]
                at += count
        half = small.shape[0] // 2
        for k in range(2):
            put(sides[0], k, 2 * size, small[k * half : (k + 1) * half, :].astype(BF), keep, send)


def added(keep, received):
    return (keep[...].astype(F32) + received[...].astype(F32)).astype(BF)


def halve_kernel(at, sides, *refs):
    keep, send = refs[-2:]
    parts = refs[:-2]
    sums = [added(parts[k], parts[k + 1]) for k in range(0, len(parts), 2)]
    total = sums[0] if len(sums) == 1 else jnp.concatenate(sums, axis=0)
    half = total.shape[0] // 2
    put(sides[at], 0, 0, total[:half], keep, send)
    put(sides[at], 1, 0, total[half:], keep, send)


def sum_kernel(mine, received, out_ref):
    out_ref[...] = added(mine, received)


def join_kernel(at, sides, mine, received, out_ref):
    half = mine.shape[0]

    @pl.when(sides[at] == 0)
    def _():
        out_ref[:half, :] = mine[...]
        out_ref[half:, :] = received[...]

    @pl.when(sides[at] != 0)
    def _():
        out_ref[:half, :] = received[...]
        out_ref[half:, :] = mine[...]


def write_mlp(low, high, up_ref, down_ref):
    down_ref[...] = low.astype(F32)
    size = down_ref.shape[1]
    for k in range(up_ref.shape[1] // size):
        span = slice(k * size, (k + 1) * size)
        up_ref[:, span] = high[span, :].astype(F32)


def write_attention(low, high, qkv_ref, out_ref):
    size = out_ref.shape[1]
    qkv_ref[0] = low[:size].astype(F32)
    qkv_ref[1] = low[size : 2 * size].astype(F32)
    qkv_ref[2] = high[:size].astype(F32)
    out_ref[...] = high[size : 2 * size].astype(F32)


def low_high(sides, mine, received):
    first = sides[0] == 0
    return jnp.where(first, mine[...], received[...]), jnp.where(first, received[...], mine[...])


def layer_result(sides, mine, received, up_ref, down_ref, qkv_ref, out_ref):
    low, high = low_high(sides, mine, received)
    cut = down_ref.shape[0]
    write_mlp(low[:cut], high[:cut], up_ref, down_ref)
    write_attention(low[cut:], high[cut:], qkv_ref, out_ref)


def mlp_result(sides, mine, received, *refs):
    write_mlp(*low_high(sides, mine, received), *refs[-2:])


def attention_result(sides, mine, received, *refs):
    qkv_ref, out_ref, small_ref = refs[-3:]
    low, high = low_high(sides, mine, received)
    write_attention(low, high, qkv_ref, out_ref)
    at = 2 * out_ref.shape[1]
    half = small_ref.shape[0] // 2
    small_ref[:half, :] = low[at:].astype(F32)
    small_ref[half:, :] = high[at:].astype(F32)


def small_kernel(mine, by_row, by_col, by_both, *outs):
    gain1, bias1, b_out, gain2, bias2, b_down, qvb, bup = outs
    count = mine.shape[0] // 2

    def split(layer, at, rows, out_at):
        own = slice(layer * count + at, layer * count + at + rows)
        other = slice(layer * count + at + rows, layer * count + at + 2 * rows)
        value = mine[own, :] + by_row[other, :]
        if layer == 0 and out_at == 0:
            value = value + (by_col[own, :] + by_both[other, :])
        return value

    for layer in range(LAYERS):
        norm = split(layer, 0, 2, 0)
        gain1[layer : layer + 1, :] = norm[0:1]
        bias1[layer : layer + 1, :] = norm[1:2]
        rest = split(layer, 4, 3, 1)
        b_out[layer : layer + 1, :] = rest[0:1]
        gain2[layer : layer + 1, :] = rest[1:2]
        bias2[layer : layer + 1, :] = rest[2:3]
        b_down[layer : layer + 1, :] = split(layer, 10, 1, 2)
        at = layer * count + 12
        qvb[layer] = mine[at : at + 2, :] + by_row[at : at + 2, :]
        last = mine[at + 2 : at + 6, :] + by_row[at + 2 : at + 6, :]
        size = last.shape[1]
        for k in range(4):
            bup[layer : layer + 1, k * size : (k + 1) * size] = last[k : k + 1]


SWAP = [(0, 1), (1, 0)]


def row_swap(operand):
    return lax.ppermute(operand, "row", SWAP)


def col_swap(operand):
    return lax.ppermute(operand, "col", SWAP)


def flipped(index, pairing):
    z, x, y = index // 8, (index // 2) % 4, index % 2
    if pairing == "za":
        z ^= 1
    elif pairing == "zb":
        z = 3 - z
    elif pairing == "xa":
        x ^= 1
    elif pairing == "xb":
        x = 3 - x
    else:
        y ^= 1
    return z * 8 + x * 2 + y


def side_of(index, pairing):
    z, x, y = index // 8, (index // 2) % 4, index % 2
    return {
        "za": (z + 1) // 2 % 2,
        "zb": z // 2,
        "xa": (x + 1) // 2 % 2,
        "xb": x // 2,
        "y": y,
    }[pairing]


def exchange(operand, pairings):
    table = [
        (dp * 2 + row, flipped(dp, pairings[row]) * 2 + row) for dp in range(32) for row in range(2)
    ]
    return lax.ppermute(operand, ("dp", "row"), table)


def my_side(pairings):
    dp = lax.axis_index("dp")
    return jnp.where(
        lax.axis_index("row") == 0, side_of(dp, pairings[0]), side_of(dp, pairings[1])
    )


Z_FIRST = [("za", "xa"), ("xa", "za"), ("zb", "xb"), ("xb", "zb"), ("y", "y")]
B_FIRST = [("zb", "xb"), ("xb", "zb"), ("za", "xa"), ("xa", "za"), ("y", "y")]


SMEM = pl.BlockSpec(memory_space=pltpu.SMEM)


class DataTotal:
    def __init__(self, order, sides, halvings):
        self.order, self.sides, self.halvings = order, sides, halvings
        self.parts, self.at = [], 0

    def start(self, keep, send):
        self.parts += [keep, exchange(send, self.order[0])]
        self.at = 1

    def step(self, after=()):
        at, count = self.at, len(self.order)
        rows = sum(part.shape[0] for part in self.parts[::2])
        width = self.parts[0].shape[1]
        if at < self.halvings:
            half = kept_of((rows // 2, width), BF)
            keep, send = call(
                partial(halve_kernel, at),
                [self.sides, *self.parts],
                [half, half],
                0,
                {0: SMEM},
                after,
            )
            pairings = self.order[at]
        elif at <= count:
            keep = send = call(sum_kernel, self.parts, [kept_of((rows, width), BF)], after=after)[0]
            pairings = self.order[at] if at < count else self.order[self.halvings - 1]
        else:
            back = self.halvings - 1 - (at - count - 1)
            keep = send = call(
                partial(join_kernel, back),
                [self.sides, *self.parts],
                [kept_of((2 * rows, width), BF)],
                0,
                {0: SMEM},
                after,
            )[0]
            pairings = self.order[back - 1]
        self.parts = [keep, exchange(send, pairings)]
        self.at += 1
        return send

    @property
    def left(self):
        return len(self.order) + self.halvings - self.at


def body(
    tokens,
    cotangent,
    ln1_gain,
    ln1_bias,
    w_qkv,
    qv_bias,
    w_out,
    b_out,
    ln2_gain,
    ln2_bias,
    w_up,
    b_up,
    w_down,
    b_down,
    seq_lengths,
    seq_owner,
    seq_offset,
):
    row = lax.axis_index("row")
    col = lax.axis_index("col")
    block, half = tokens.shape
    part = block // 2
    rows = block
    width = 2 * half
    hidden_part = w_up.shape[2]

    def split_input(operand):
        own = lax.dynamic_slice_in_dim(operand, row * part, part, 0)
        sent = lax.dynamic_slice_in_dim(operand, (1 - row) * part, part, 0)
        received = row_swap(sent)
        across = col_swap(jnp.concatenate([own, received], axis=1))
        return own, received, across

    token_parts = split_input(tokens)
    params = jnp.concatenate([ln1_gain, ln1_bias, b_out, ln2_gain, ln2_bias, b_down], axis=0)
    params = jnp.concatenate([params, row_swap(params)], axis=1)
    wq = jnp.transpose(w_qkv, (0, 2, 1, 3))
    wq_oth = row_swap(wq)
    wo_oth = row_swap(w_out)
    wu_oth = row_swap(w_up)
    wd_oth = row_swap(w_down)
    wc_own = col_swap(lax.optimization_barrier((w_out, token_parts[2]))[0])
    wc_oth = row_swap(wc_own)
    cot_parts = split_input(cotangent)
    bup = b_up[:, None, :]
    info = jnp.stack(
        [
            lax.axis_index("dp"),
            col * block + row * part,
            (1 - col) * block + row * part,
            col * block + (1 - row) * part,
            (1 - col) * block + (1 - row) * part,
        ]
    ).astype(jnp.int32)
    seqs = (info, seq_lengths[None, :], seq_owner[None, :], seq_offset[None, :])
    smem = SMEM
    head_width = w_qkv.shape[3]
    full_kept = kept_of((rows, width), BF)
    act_kept = kept_of((rows, half), BF)
    stream_kept = kept_of((rows, width), F32)
    wide_kept = kept_of((rows, hidden_part), BF)

    kept = []
    x1 = y_down = y_down_rec = None
    for l in range(LAYERS):
        outs = [stream_kept, act_kept, act_kept, act_kept, full_kept]
        if l == 0:
            ins = [*token_parts, params, qv_bias, wq, wq_oth]
            kernel = partial(first_kernel, l)
        else:
            ins = [x1, y_down, y_down_rec, params, qv_bias, wq, wq_oth]
            kernel = partial(next_kernel, l)
        spec = {k: layer_spec(ins[k], l) for k in (4, 5, 6)}
        x, a_own, a_oth, q, kv = call(kernel, ins, outs, 2 * rows * width * 3 * half, spec)
        kv_rec = row_swap(kv)
        a_rec = row_swap(a_oth)
        ins = [*seqs, q, kv, kv_rec]
        o, lse = call(
            attend_kernel,
            ins,
            [act_kept, kept_of((rows, 128), F32)],
            2 * rows * width * half * 2,
            {0: smem},
        )
        o_across = col_swap(o)
        o_rec = row_swap(o)
        ins = [x, o, o_across, params, w_out, wo_oth, wc_own, wc_oth]
        ins += [bup, w_up, wu_oth, w_down, wd_oth]
        spec = {k: layer_spec(ins[k], l) for k in range(4, 13)}
        x1, m_own, m_oth, h, gp, y_down = call(
            partial(mlp_kernel, l),
            ins,
            [stream_kept, act_kept, act_kept, wide_kept, wide_kept, full_kept],
            4 * rows * width * hidden_part,
            spec,
        )
        m_rec = row_swap(m_oth)
        h_rec = row_swap(h)
        if l < LAYERS - 1:
            y_down_rec = col_swap(y_down)
        kept.append((x, a_own, a_rec, q, kv, kv_rec, o, o_rec, lse, x1, m_own, m_rec, h, h_rec, gp))

    y_last = col_swap(y_down[part:])
    out_rows = x1[:part] + (
        y_down[:part].astype(F32) + y_last.astype(F32) + params[-1:, :]
    )
    out_other = row_swap(out_rows[:, half:])
    out_own = out_rows[:, :half]

    def by_row(own, other):
        return jnp.where(
            row == 0, jnp.concatenate([own, other]), jnp.concatenate([other, own])
        )

    out_act = by_row(out_own, out_other)

    flops = rows * width * half
    z_sides = jnp.stack([my_side(p) for p in Z_FIRST]).astype(jnp.int32)
    b_sides = jnp.stack([my_side(p) for p in B_FIRST]).astype(jnp.int32)

    def mlp_total(layer, sides, gy_own, gy_rec, du, du_rec, after=()):
        h, h_rec, m_own, m_rec = (kept[layer][k] for k in (12, 13, 10, 11))
        return call(
            mlp_grads,
            [sides, h, h_rec, gy_own, gy_rec, m_own, m_rec, du, du_rec],
            [kept_of((4 * half, half), BF)] * 2,
            4 * rows * half * half * 8,
            {0: smem},
            after,
        )

    def attention_total(layer, sides, ins, smalls=(), after=()):
        a_own, a_rec, o, o_rec = (kept[layer][k] for k in (1, 2, 6, 7))
        ga_own, ga_rec, dq, dq_rec, dkv, dkv_rec = ins
        extra = SMALL_ROWS // 2 if smalls else 0
        return call(
            attention_grads,
            [sides, o, o_rec, ga_own, ga_rec, a_own, a_rec, dq, dq_rec, dkv, dkv_rec, *smalls],
            [kept_of((2 * half + extra, half), BF)] * 2,
            4 * rows * half * half * 4,
            {0: smem},
            after,
            scratch=[pltpu.VMEM((SMALL_ROWS, half), F32)],
        )

    def mlp_stage(layer, kernel, ins, outs, after):
        first = len(ins)
        ins = ins + [kept[layer][14], w_up, wu_oth, w_down, wd_oth]
        spec = {k: layer_spec(ins[k], layer) for k in range(first + 1, first + 5)}
        return call(kernel, ins, outs, 4 * flops * 4, spec, after)

    def attend_stage(layer, g, dm, dm_rec, after):
        x1, q, kv, kv_rec, lse = (kept[layer][k] for k in (9, 3, 4, 5, 8))
        ins = [*seqs, g, dm, dm_rec, x1, params, w_out, wo_oth, q, kv, kv_rec, lse]
        spec = {0: smem, 9: layer_spec(w_out, layer), 10: layer_spec(wo_oth, layer)}
        return call(
            partial(attend_back_kernel, layer),
            ins,
            [
                stream_kept,
                act_kept,
                act_kept,
                act_kept,
                full_kept,
                full_kept,
                shape_of((3, width), F32),
            ],
            6 * flops,
            spec,
            after,
        )

    def project_stage(layer, kernel, ins, outs, after=()):
        ins = [*ins[:3], wq, wq_oth, *ins[3:]]
        spec = {3: layer_spec(wq, layer), 4: layer_spec(wq_oth, layer)}
        outs = [full_kept, shape_of((2, half), F32)] + outs
        return call(kernel, ins, outs, 6 * flops, spec, after)

    outs = [
        pltpu.HBM((rows, width), F32),
        pltpu.HBM((rows, half), BF),
        pltpu.HBM((rows, half), BF),
        pltpu.HBM((rows, hidden_part), BF),
        full_kept,
        shape_of((1, width), F32),
        shape_of((hidden_part // half, half), F32),
    ]
    layer_one = DataTotal(Z_FIRST, z_sides, 3)
    mlp_zero = DataTotal(B_FIRST, b_sides, 3)
    attention_zero = DataTotal(Z_FIRST, z_sides, 2)
    g, gy_own, gy_oth, du, dm, s_down1, s_up1 = mlp_stage(
        1, last_back_kernel, list(cot_parts), outs, ()
    )
    dm_rec, gy_rec, du_rec = col_swap(dm), row_swap(gy_oth), row_swap(du)
    keep, send = mlp_total(1, z_sides, gy_own, gy_rec, du, du_rec)
    layer_one.start(keep, send)
    g1, ga_own, ga_oth, dq, dkv, dkv_oth, s_att1 = attend_stage(1, g, dm, dm_rec, (send,))
    dkv_rec, ga_rec, dq_rec = row_swap(dkv_oth), row_swap(ga_oth), row_swap(dq)
    dkv_total, s_qv1, da = project_stage(1, project_back_kernel, [dq, dkv, dkv_rec], [full_kept])
    da_rec, dkv_total_rec = col_swap(da), row_swap(dkv_total)
    keep, send = attention_total(
        1, z_sides, [ga_own, ga_rec, dq, dq_rec, dkv_total, dkv_total_rec]
    )
    layer_one.start(keep, send)
    s_ln1, g, gy_own, gy_oth, du, dm, s_down0, s_up0 = mlp_stage(
        0,
        partial(next_back_kernel, 0),
        [g1, da, da_rec, kept[1][0], params],
        [shape_of((2, width), F32)] + outs,
        (send,),
    )
    dm_rec, gy_rec, du_rec = col_swap(dm), row_swap(gy_oth), row_swap(du)
    sent = layer_one.step((dm,))
    keep, send = mlp_total(0, b_sides, gy_own, gy_rec, du, du_rec, (sent,))
    mlp_zero.start(keep, send)
    g1, ga_own, ga_oth, dq, dkv, dkv_oth, s_att0 = attend_stage(0, g, dm, dm_rec, (send,))
    dkv_rec, ga_rec, dq_rec = row_swap(dkv_oth), row_swap(ga_oth), row_swap(dq)
    dkv_total, s_qv0, da_keep, da_send, s_ln0 = project_stage(
        0,
        project_end_kernel,
        [dq, dkv, dkv_rec, kept[0][0]],
        [kept_of((part, width), BF)] * 2 + [shape_of((2, width), F32)],
    )
    da_rec, dkv_total_rec = col_swap(da_send), row_swap(dkv_total)
    smalls = [s_ln0, s_att0, s_down0, s_qv0, s_up0, s_ln1, s_att1, s_down1, s_qv1, s_up1]
    keep, send = attention_total(
        0, z_sides, [ga_own, ga_rec, dq, dq_rec, dkv_total, dkv_total_rec], smalls
    )
    attention_zero.start(keep, send)
    sent = layer_one.step((send,))
    sent = mlp_zero.step((sent,))
    grad_own, grad_oth = call(
        partial(end_back_kernel, 0),
        [g1, da_keep, da_rec, kept[0][0], params],
        [kept_of((part, half), F32)] * 2,
        after=(sent,),
    )
    grad_tokens = by_row(grad_own, row_swap(grad_oth))
    sent = grad_own
    while attention_zero.left > 0 or mlp_zero.left > 0 or layer_one.left > 0:
        for total in (attention_zero, layer_one, mlp_zero):
            if total.left > 0:
                sent = total.step((sent,))

    def result(kernel, total, layer, shapes, before, extra=()):
        ins = [total.sides, *total.parts, *before]
        specs = {0: smem}
        for k in range(3, len(ins)):
            specs[k] = pl.BlockSpec(memory_space=pl.ANY)
        aliases = {3 + k: k for k in range(len(before))}
        outs = [(shape, layer_spec(shape, layer)) for shape in shapes] + list(extra)
        return call(kernel, ins, outs, 0, specs, aliases=aliases)

    up, down, qkv, out = result(
        layer_result,
        layer_one,
        1,
        [kept_of(x.shape, F32) for x in (w_up, w_down, wq, w_out)],
        [],
    )
    grad_up, grad_down = result(
        mlp_result, mlp_zero, 0, [kept_of(x.shape, F32) for x in (w_up, w_down)], [up, down]
    )
    grad_qkv, grad_out, small = result(
        attention_result,
        attention_zero,
        0,
        [kept_of(x.shape, F32) for x in (wq, w_out)],
        [qkv, out],
        [shape_of((SMALL_ROWS, half), F32)],
    )
    grad_qkv = jnp.transpose(grad_qkv, (0, 2, 1, 3))
    small = small[:36]
    across = lax.ppermute(small, ("row", "col"), [(k, 3 - k) for k in range(4)])
    vector = shape_of((LAYERS, half), F32)
    g_gain1, g_bias1, g_bout, g_gain2, g_bias2, g_bdown, g_qvb, g_bup = call(
        small_kernel,
        [small, row_swap(small), col_swap(small), across],
        [vector] * 6 + [shape_of(qv_bias.shape, F32), shape_of(b_up.shape, F32)],
    )
    return (
        out_act,
        grad_tokens,
        g_gain1,
        g_bias1,
        grad_qkv,
        g_qvb,
        grad_out,
        g_bout,
        g_gain2,
        g_bias2,
        grad_up,
        g_bup,
        grad_down,
        g_bdown,
    )


def solution(mesh):
    in_specs = (
        P(("dp", "col"), "row"),
        P(("dp", "col"), "row"),
        P(None, "row"),
        P(None, "row"),
        P(None, "row", None, "col"),
        P(None, None, "col"),
        P(None, "col", "row"),
        P(None, "row"),
        P(None, "row"),
        P(None, "row"),
        P(None, "row", "col"),
        P(None, "col"),
        P(None, "col", "row"),
        P(None, "row"),
        P(),
        P(),
        P(),
    )
    out_specs = (
        P(("dp", "col"), "row"),
        P(("dp", "col"), "row"),
        P(None, "row"),
        P(None, "row"),
        P(None, "row", None, "col"),
        P(None, None, "col"),
        P(None, "col", "row"),
        P(None, "row"),
        P(None, "row"),
        P(None, "row"),
        P(None, "row", "col"),
        P(None, "col"),
        P(None, "col", "row"),
        P(None, "row"),
    )
    return jax.shard_map(body, mesh=mesh, in_specs=in_specs, out_specs=out_specs, check_vma=False)
```
